512 devices in a mesh: tm: 32 (over x, y, core), space: 16 (over z).
Axes of the slice: x: 4, y: 4, z: 16, core: 2. Of those that a mesh axis runs over, the one named last changes fastest.
Arguments:
- initial_state: float32 [64, 2048], P(None, 'space'), may hold values from -6 to 6
- forcing: float32 [128, 64, 2048], P('tm', None, 'space'), may hold values from -4 to 4
- coarse_gain: float32 [32, 64, 2048], P('tm', None, 'space'), may hold values from 0.05 to 1, as said below
- block_inverse: float32 [64, 64, 2048], P(None, None, 'space'), may hold values from -0.25 to 1.1
- face_blocks: float32 [6, 64, 64], replicated, may hold values from -0.1875 to 0.1875
- neighbor: int32 [6, 2048], P(None, 'space'), may hold values from -1 to 255, as said below
- send_rows: int32 [2, 1024], P(None, 'space'), may hold values from 0 to 127, as said below
Outputs:
- coarse_end: float32 [32, 64, 2048], P('tm', None, 'space')
- residual: float32 [32, 64, 2048], P('tm', None, 'space')
The draws below stay inside these ranges and needn't reach their ends.
Inputs may be any that keep to these rules, and one draw needn't show every extreme that they name: `neighbor`: for face f (-x, +x, -y, +y, -z, +z) of the element in local column e, the local column of its neighbour in the extended field of its partition; -1 where the face lies on the domain's side along x or y. `send_rows`: row 0 lists the local columns of a partition's lowest element layer, row 1 those of its highest, in the same order of x and y. `coarse_gain`: Positive, below one.
All inputs are finite; a program needn't handle non-finite values.
Results may differ from the reference program's by a relative error of at most 0.00014.
Values sent between devices are 32-bit elements; how exact they have to be, the bound alone decides.
No kernel may reach another device: no remote copies, remote signals or barrier semaphores. Data moves between devices by JAX's collectives and lax.ppermute only.
A program may use at most 64 MiB of HBM per device.

```python
import jax
import jax.numpy as jnp
from jax import lax

BLOCK_VALUES = 64
GX = 8
GY = 8
STEPS = 4
SWEEPS = 2
ITERS = 2
E_DEV = 128
ELEMENT_TOTAL = 2048
TIME_SLICES = 32
NF = 128
N_SPACE = 16


def grid_slots(key):
    random_key_array = jax.random.split(key, N_SPACE)
    return jax.vmap(lambda part_key: jax.random.permutation(part_key, E_DEV))(random_key_array).astype(jnp.int32)


def draw_neighbor(key, part):
    slot_table = grid_slots(key)
    layer_size = GX * GY
    grid_cell = jnp.argsort(slot_table, axis=1, stable=True).astype(jnp.int32)
    z_level = grid_cell // layer_size
    within = grid_cell % layer_size
    y_index = within // GX
    x_index = within % GX

    def lookup(target):
        return jnp.take_along_axis(slot_table, jnp.clip(target, 0, E_DEV - 1), axis=1)
    minus_x = jnp.where(x_index > 0, lookup(grid_cell - 1), -1)
    plus_x = jnp.where(x_index < GX - 1, lookup(grid_cell + 1), -1)
    minus_y = jnp.where(y_index > 0, lookup(grid_cell - GX), -1)
    plus_y = jnp.where(y_index < GY - 1, lookup(grid_cell + GX), -1)
    minus_z = jnp.where(z_level > 0, lookup(grid_cell - layer_size), E_DEV + within)
    plus_z = jnp.where(z_level < 1, lookup(grid_cell + layer_size), E_DEV + layer_size + within)
    stacked = jnp.stack([minus_x, plus_x, minus_y, plus_y, minus_z, plus_z], axis=0)
    return stacked.reshape(6, N_SPACE * E_DEV).astype(jnp.int32)


def draw_send_rows(key, part):
    slot_table = grid_slots(key)
    layer_size = GX * GY
    stacked = jnp.stack([slot_table[:, :layer_size], slot_table[:, layer_size:]], axis=0)
    return stacked.reshape(2, N_SPACE * layer_size).astype(jnp.int32)


def draw_block_inverse(key, part):
    key = jax.random.fold_in(key, 3)
    random_key_array = jax.random.split(key, 2)
    shape_full = (BLOCK_VALUES, BLOCK_VALUES, ELEMENT_TOTAL)
    elem_scale = jnp.exp(jax.random.uniform(random_key_array[0], (1, 1, ELEMENT_TOTAL), minval=jnp.log(0.5), maxval=jnp.log(0.9)))
    noise_part = jnp.clip(jax.random.normal(random_key_array[1], shape_full), -4.0, 4.0)
    row_index = lax_iota(BLOCK_VALUES)[:, None, None]
    col_index = lax_iota(BLOCK_VALUES)[None, :, None]
    identity = (row_index == col_index).astype(jnp.float32)
    return (elem_scale * (identity + 0.05 * noise_part)).astype(jnp.float32)


def lax_iota(count):
    return jnp.arange(count, dtype=jnp.int32)


def draw_coarse_gain(key, part):
    key = jax.random.fold_in(key, 5)
    random_key_array = jax.random.split(key, 4)
    rate_low = 0.1 / TIME_SLICES
    rate_high = 1.5
    damping_rate = jnp.exp(jax.random.uniform(random_key_array[0], (1, BLOCK_VALUES, ELEMENT_TOTAL), minval=jnp.log(rate_low), maxval=jnp.log(rate_high)))
    random_perturbation = jax.random.uniform(random_key_array[1], (TIME_SLICES, BLOCK_VALUES, ELEMENT_TOTAL), minval=0.5, maxval=1.5)
    spike_event = jax.random.uniform(random_key_array[2], (TIME_SLICES, BLOCK_VALUES, ELEMENT_TOTAL)) < 2.0 / TIME_SLICES
    spike_depth = jax.random.uniform(random_key_array[3], (TIME_SLICES, BLOCK_VALUES, ELEMENT_TOTAL), minval=0.5, maxval=0.8)
    gain_factors = jnp.exp(-damping_rate * random_perturbation) * jnp.where(spike_event, spike_depth, 1.0)
    return gain_factors.astype(jnp.float32)


def shard_levels(own_key, extent, pieces, smallest, top_value):
    factor_of = 1.0
    for axis_at, blocks in pieces:
        steps = jax.random.uniform(jax.random.fold_in(jax.random.fold_in(own_key, 6), axis_at), (blocks,), jnp.float32, smallest / len(pieces), top_value / len(pieces))
        factor_of = factor_of * jnp.repeat(jnp.exp(steps), extent[axis_at] // blocks).reshape((-1,) + (1,) * (len(extent) - 1 - axis_at))
    return factor_of


def bell_draw(stream_key, extent, width, reach, pieces=(), kind=jnp.bfloat16):
    drawn = jax.random.normal(stream_key, extent, jnp.float32) * width
    if len(pieces) > 0:
        drawn = shard_levels(stream_key, extent, pieces, -0.22, 0.18) * drawn
    return jnp.clip(drawn, min=-reach, max=reach).astype(kind)


def setup_inputs(seed: int = 0) -> dict:
    arg_keys = jax.random.split(jax.random.key(seed), 8)
    initial_state = bell_draw(arg_keys[0], (BLOCK_VALUES, ELEMENT_TOTAL), 1.0, 6.0, ((1, 16),), jnp.float32)
    forcing = bell_draw(arg_keys[1], (NF, BLOCK_VALUES, ELEMENT_TOTAL), 0.5, 4.0, ((0, 32), (2, 16)), jnp.float32)
    coarse_gain = draw_coarse_gain(jax.random.fold_in(arg_keys[7], 71), 0)
    block_inverse = draw_block_inverse(jax.random.fold_in(arg_keys[7], 71), 0)
    face_blocks = bell_draw(arg_keys[4], (6, BLOCK_VALUES, BLOCK_VALUES), (18 * BLOCK_VALUES) ** -0.5, 0.1875, (), jnp.float32)
    neighbor = draw_neighbor(jax.random.fold_in(arg_keys[7], 71), 0)
    send_rows = draw_send_rows(jax.random.fold_in(arg_keys[7], 71), 0)
    return {"initial_state": initial_state, "forcing": forcing, "coarse_gain": coarse_gain, "block_inverse": block_inverse, "face_blocks": face_blocks, "neighbor": neighbor, "send_rows": send_rows}


HIGHEST_PRECISION = lax.Precision.HIGHEST


def extend_all(field_now, send_rows):
    nt, values, parts, elems = field_now.shape
    send_table = send_rows.reshape(2, N_SPACE, -1)
    layer_size = send_table.shape[2]
    shape_rows = (nt, values, parts, layer_size)
    bottom = jnp.take_along_axis(field_now, jnp.broadcast_to(send_table[0][None, None], shape_rows), axis=3)
    upper_rows = jnp.take_along_axis(field_now, jnp.broadcast_to(send_table[1][None, None], shape_rows), axis=3)
    zero_rows = jnp.zeros((nt, values, 1, layer_size), jnp.float32)
    below_rows = jnp.concatenate([zero_rows, upper_rows[:, :, :-1]], axis=2)
    above_rows = jnp.concatenate([bottom[:, :, 1:], zero_rows], axis=2)
    return jnp.concatenate([field_now, below_rows, above_rows], axis=3)


def coupling(field_now, face_blocks, neighbor, send_rows):
    extended = extend_all(field_now, send_rows)
    face_sum = jnp.zeros_like(field_now)
    for face in range(6):
        gather_index = jnp.broadcast_to(jnp.maximum(neighbor[face], 0)[None, None], field_now.shape)
        picked = jnp.take_along_axis(extended, gather_index, axis=3)
        face_valid = (neighbor[face] >= 0).astype(jnp.float32)
        picked = picked * face_valid[None, None]
        face_sum = face_sum + jnp.einsum("ij,tjse->tise", face_blocks[face], picked, precision=HIGHEST_PRECISION)
    return face_sum


def reference(initial_state, forcing, coarse_gain, block_inverse, face_blocks, neighbor, send_rows):
    values = initial_state.shape[0]
    nt = coarse_gain.shape[0]
    parts = N_SPACE
    elems = initial_state.shape[1] // parts
    start_field = initial_state.reshape(values, parts, elems)
    sources = forcing.reshape(nt, STEPS, values, parts, elems)
    gain_factors = coarse_gain.reshape(nt, values, parts, elems)
    inverse = block_inverse.reshape(values, values, parts, elems)
    adjacency = neighbor.reshape(6, parts, elems)

    def apply_inverse(vector):
        return jnp.einsum("ijse,tjse->tise", inverse, vector, precision=HIGHEST_PRECISION)

    coarse = jnp.zeros((nt, values, parts, elems), jnp.float32)
    residual = coarse
    for iteration in range(ITERS):
        field_now = jnp.concatenate([start_field[None], coarse[:-1]], axis=0)
        for step_index in range(STEPS):
            right_side = field_now + sources[:, step_index]
            field_now = apply_inverse(right_side)
            for sweep_index in range(SWEEPS):
                field_now = apply_inverse(right_side - coupling(field_now, face_blocks, adjacency, send_rows))
        residual = field_now - coarse

        def chain(running, pair):
            running = pair[0] * running + pair[1]
            return running, running

        zero_field = jnp.zeros((values, parts, elems), jnp.float32)
        running, correction = lax.scan(chain, zero_field, (gain_factors, residual))
        coarse = coarse + correction
    shape_out = (nt, values, parts * elems)
    return coarse.reshape(shape_out), residual.reshape(shape_out)
```

```python
import functools

import jax
import jax.numpy as jnp
from jax import lax
from jax.experimental import pallas as pl
from jax.experimental.pallas import tpu as pltpu
from jax.sharding import Mesh, PartitionSpec as P


VALUES = 64
LANES = 128
HALF = 64
STEPS = 4
STAGES = 2 * STEPS
HIGHEST = lax.Precision.HIGHEST
F32 = jnp.float32
FIELD = (VALUES, LANES)


def vmem(x):
    return pltpu.with_memory_space_constraint(x, pltpu.VMEM)


def call(kernel, name, outs, *args, keep=True, flops=1 << 22):
    whole = pl.BlockSpec(memory_space=pltpu.VMEM)
    shapes = tuple(
        pltpu.VMEM(shape, dtype) if keep else jax.ShapeDtypeStruct(shape, dtype)
        for shape, dtype in outs
    )
    return pl.pallas_call(
        kernel,
        out_shape=shapes,
        in_specs=[whole] * len(args),
        out_specs=(whole,) * len(shapes),
        scratch_shapes=[pltpu.VMEM(FIELD, F32)],
        cost_estimate=pl.CostEstimate(flops=flops, bytes_accessed=1 << 20, transcendentals=0),
        compiler_params=pltpu.CompilerParams(vmem_limit_bytes=16 << 20),
        name=name,
    )(*args)


def low_half():
    return lax.broadcasted_iota(jnp.int32, FIELD, 1) < HALF


def swap_halves(x):
    return pltpu.roll(x, HALF, 1)


def columns(x, index):
    return jnp.take_along_axis(x, jnp.broadcast_to(index, x.shape), axis=1)


def twice(row):
    return jnp.concatenate([row, row], axis=1)


def layer_rows(send_ref, core):
    lowest, highest = send_ref[0:1, :], send_ref[1:2, :]
    mine = jnp.where(core == 0, lowest, highest)
    other = jnp.where(core == 0, highest, lowest)
    return twice(mine), twice(other)


def apply_inverse(inverse_ref, scratch, vector):
    scratch[...] = vector
    sums = [None, None]
    for j in range(VALUES):
        term = inverse_ref[j] * scratch[j : j + 1, :]
        sums[j % 2] = term if sums[j % 2] is None else sums[j % 2] + term
    return sums[0] + sums[1]


def coupling(field, far, near, index, valid, faces):
    picked = [
        columns(field, index[f : f + 1, :]) * jnp.broadcast_to(valid[f : f + 1, :], FIELD)
        for f in range(4)
    ]
    stacked = jnp.concatenate(picked + [far, near], axis=0)
    return jnp.dot(faces, stacked, precision=HIGHEST, preferred_element_type=F32)


def share_kernel(send_ref, forcing_ref, gain_ref, state_ref, own_ref, out_ref, start_ref, _):
    core = lax.axis_index("c")
    mine, other = layer_rows(send_ref, core)
    low = low_half()
    fields = [forcing_ref[m] for m in range(STEPS)] + [gain_ref[0]]
    for m, field in enumerate(fields):
        own_ref[m] = columns(field, mine)
    for m in range(0, STEPS, 2):
        out_ref[m // 2] = jnp.where(low, columns(fields[m], other), columns(fields[m + 1], other))
    out_ref[STEPS // 2] = columns(fields[STEPS], other)
    start_ref[...] = columns(state_ref[...], mine)


def tables_kernel(
    send_ref, neighbor_ref, inverse_ref, blocks_ref, index_ref, valid_ref, place_ref, faces_ref,
    table_ref, _
):
    core = lax.axis_index("c")
    mine, _other = layer_rows(send_ref, core)
    order = jnp.concatenate([send_ref[0:1, :], send_ref[1:2, :]], axis=1)
    down = jnp.transpose(jnp.broadcast_to(order.astype(F32), (LANES, LANES)))
    across = lax.broadcasted_iota(jnp.int32, (LANES, LANES), 1).astype(F32)
    at = lax.broadcasted_iota(jnp.int32, (LANES, LANES), 0).astype(F32)
    place = jnp.sum(jnp.where(down == across, at, 0.0), axis=0, keepdims=True).astype(jnp.int32)
    place = jnp.broadcast_to(place, (8, LANES))
    place_ref[...] = place
    pad = jnp.zeros((2, LANES), jnp.int32)
    local = columns(jnp.concatenate([neighbor_ref[...], pad], axis=0), mine)
    valid_ref[...] = (local >= 0).astype(F32)
    lane = lax.broadcasted_iota(jnp.int32, (8, LANES), 1)
    spot = columns(place, jnp.clip(local, 0, LANES - 1))
    index_ref[...] = jnp.bitwise_and(spot, HALF - 1) + jnp.where(lane < HALF, 0, HALF)
    for f in range(4):
        faces_ref[:, f * VALUES : (f + 1) * VALUES] = blocks_ref[f]
    faces_ref[:, 4 * VALUES : 5 * VALUES] = jnp.where(core == 0, blocks_ref[4], blocks_ref[5])
    faces_ref[:, 5 * VALUES : 6 * VALUES] = jnp.where(core == 0, blocks_ref[5], blocks_ref[4])
    for j in range(VALUES):
        table_ref[j] = columns(inverse_ref[pl.ds(j, VALUES, stride=VALUES), :], mine)


def first_kernel(
    own_ref, got_ref, start_ref, table_ref, sources_ref, gain_ref, pair_ref, right_ref, scratch
):
    core = lax.axis_index("c")
    low = low_half()
    is_own = low == (core == 0)
    for m in range(STEPS + 1):
        got = got_ref[m // 2]
        turned = swap_halves(got)
        if m % 2 == 0:
            other = jnp.where(core == 0, turned, got)
        else:
            other = jnp.where(core == 0, got, turned)
        value = jnp.where(is_own, own_ref[m], other)
        if m < STEPS:
            sources_ref[m] = value
        else:
            gain_ref[...] = value
    first = jnp.logical_and(low, lax.axis_index("q") == 0)
    right = jnp.where(first, start_ref[...], 0.0) + sources_ref[0]
    right_ref[...] = right
    pair_ref[0] = jnp.zeros(FIELD, F32)
    pair_ref[1] = apply_inverse(table_ref, scratch, right)


def advance(plan, refs, sourced, scratch):
    (pair_ref, right_ref, far_ref, near_ref, index_ref, valid_ref, faces_ref, table_ref, sources_ref,
     pair_out, right_out) = refs
    active, stages = plan
    core = lax.axis_index("c")

    @pl.when(core == active)
    def _run():
        index, valid, faces = index_ref[...], valid_ref[...], faces_ref[...]
        field = pair_ref[1]
        right = right_ref[...]
        for stage, slot in stages:
            pair_out[0] = field
            summed = coupling(field, far_ref[slot], near_ref[slot], index, valid, faces)
            field = apply_inverse(table_ref, scratch, right - summed)
            if stage % 2 == 1 and stage < STAGES - 1:
                right = field
                if sourced:
                    right = right + sources_ref[(stage + 1) // 2]
                field = apply_inverse(table_ref, scratch, right)
        pair_out[1] = field
        right_out[...] = right

    @pl.when(core != active)
    def _keep():
        pair_out[...] = pair_ref[...]
        right_out[...] = right_ref[...]


def advance_kernel(plan, sourced, *refs):
    advance(plan, refs[:-1], sourced, refs[-1])


def ends_kernel(plan, count, *refs):
    (*inner, gain_ref, pair_out, right_out, chunk_ref, scratch) = refs
    advance(plan, (*inner, pair_out, right_out), True, scratch)
    low = low_half()
    gain, end = gain_ref[...], pair_out[1]
    summed = gain * swap_halves(end) + end
    chunk = jnp.where(low, gain * swap_halves(gain), summed)
    for q in range(count):
        chunk_ref[q] = chunk


def ends_last_kernel(plan, count, *refs):
    (*inner, gain_ref, shift_ref, pair_out, right_out, residual_ref, chunk_ref, scratch) = refs
    advance(plan, (*inner, pair_out, right_out), False, scratch)
    gain = gain_ref[...]
    residual = pair_out[1] - gain * shift_ref[...]
    residual_ref[...] = residual
    summed = gain * swap_halves(residual) + residual
    low = low_half()[:HALF // 2]
    chunk = jnp.where(low, swap_halves(summed)[: VALUES // 2], summed[VALUES // 2 :])
    for q in range(count):
        chunk_ref[q] = chunk


def chained(count, before, gain, residual):
    before = jnp.where(low_half(), swap_halves(before), before)
    return jnp.where(low_half(), before, swap_halves(gain * before + residual))


def restart_kernel(count, all_ref, end_ref, gain_ref, table_ref, shift_ref, coarse_ref, pair_ref, scratch):
    mine = lax.axis_index("q")
    before = jnp.zeros(FIELD, F32)
    for q in range(count):
        chunk = all_ref[q]
        before = jnp.where(q < mine, swap_halves(chunk) * before + chunk, before)
    gain, end = gain_ref[...], end_ref[1]
    shift = chained(count, before, gain, end)
    shift_ref[...] = shift
    coarse_ref[...] = gain * shift + end
    pair_ref[0] = jnp.zeros(FIELD, F32)
    pair_ref[1] = apply_inverse(table_ref, scratch, shift)


def finish_kernel(count, all_ref, gains_ref, residual_ref, gain_ref, coarse_ref, end_ref, out_ref, _):
    core = lax.axis_index("c")
    mine = lax.axis_index("q")
    low = low_half()
    before = jnp.zeros(FIELD, F32)
    for q in range(count):
        chunk = all_ref[q]
        summed = jnp.concatenate([swap_halves(chunk), chunk], axis=0)
        before = jnp.where(q < mine, swap_halves(gains_ref[q]) * before + summed, before)
    gain, residual = gain_ref[...], residual_ref[...]
    shift = chained(count, before, gain, residual)
    end = coarse_ref[...] + (gain * shift + residual)
    end_ref[...] = end
    out_ref[...] = jnp.where(
        core == 0,
        jnp.where(low, swap_halves(end), residual),
        jnp.where(low, end, swap_halves(residual)),
    )


def output_kernel(end_ref, residual_ref, got_ref, place_ref, end_out, residual_out, _):
    core = lax.axis_index("c")
    low = low_half()
    got = got_ref[...]
    turned = swap_halves(got)
    end, residual = end_ref[...], residual_ref[...]
    end = jnp.where(core == 0, jnp.where(low, end, turned), jnp.where(low, got, end))
    residual = jnp.where(
        core == 0, jnp.where(low, residual, got), jnp.where(low, turned, residual)
    )
    place = place_ref[0:1, :]
    end_out[0] = columns(end, place)
    residual_out[0] = columns(residual, place)


def plans():
    yield 1, [(0, 1)]
    for half in range(2, STAGES + 1):
        yield half % 2, [(half - 2, 0), (half - 1, 1)]
    yield (STAGES + 1) % 2, [(STAGES - 1, 0)]


def body(count, depth, initial_state, forcing, coarse_gain, block_inverse, face_blocks, neighbor, send_rows):
    def swap_cores(x):
        return lax.ppermute(x, "c", [(0, 1), (1, 0)])

    def halo(x, to):
        if to == 1:
            across = [(z + 1, depth + z) for z in range(depth - 1)]
        else:
            across = [(depth + z, z + 1) for z in range(depth - 1)]
        far = lax.ppermute(x, ("c", "space"), across)
        near = lax.ppermute(x, "c", [(1 - to, to)])
        return vmem(far), vmem(near)

    field, pair_shape = (FIELD, F32), ((2,) + FIELD, F32)
    own, sent, start = call(
        share_kernel, "share",
        [((STEPS + 1,) + FIELD, F32), ((STEPS // 2 + 1,) + FIELD, F32), field],
        send_rows, forcing, coarse_gain, initial_state,
    )
    got = swap_cores(sent)
    index, valid, place, faces, table = call(
        tables_kernel, "tables",
        [((8, LANES), jnp.int32), ((8, LANES), F32), ((8, LANES), jnp.int32),
         ((VALUES, 6 * VALUES), F32), ((VALUES,) + FIELD, F32)],
        send_rows, neighbor, vmem(block_inverse.reshape(VALUES * VALUES, LANES)), face_blocks,
    )
    index, valid, place, faces, table = map(vmem, (index, valid, place, faces, table))
    sources, gain, pair, right = call(
        first_kernel, "first", [((STEPS,) + FIELD, F32), field, pair_shape, field],
        vmem(own), vmem(got), vmem(start), table,
    )
    sources, gain = vmem(sources), vmem(gain)
    half_phases = list(plans())

    def inner(pair, right, to):
        pair, right = vmem(pair), vmem(right)
        far, near = halo(pair, to)
        return pair, right, far, near, index, valid, faces, table, sources

    for plan in half_phases[:-1]:
        pair, right = call(
            functools.partial(advance_kernel, plan, True), "advance", [pair_shape, field],
            *inner(pair, right, plan[0]),
        )
    plan = half_phases[-1]
    pair, _, chunk = call(
        functools.partial(ends_kernel, plan, count), "ends",
        [pair_shape, field, ((count,) + FIELD, F32)], *inner(pair, right, plan[0]), gain,
    )
    gathered = vmem(lax.all_to_all(chunk, "q", 0, 0))
    shift, coarse, pair = call(
        functools.partial(restart_kernel, count), "restart", [field, field, pair_shape],
        gathered, vmem(pair), gain, table,
    )
    right = shift = vmem(shift)
    for plan in half_phases[:-1]:
        pair, right = call(
            functools.partial(advance_kernel, plan, False), "advance", [pair_shape, field],
            *inner(pair, right, plan[0]),
        )
    plan = half_phases[-1]
    _, _, residual, chunk = call(
        functools.partial(ends_last_kernel, plan, count), "ends",
        [pair_shape, field, field, ((count, VALUES // 2, LANES), F32)],
        *inner(pair, right, plan[0]), gain, shift,
    )
    sums = vmem(lax.all_to_all(chunk, "q", 0, 0))
    residual = vmem(residual)
    end, sent = call(
        functools.partial(finish_kernel, count), "finish", [field, field],
        sums, gathered, residual, gain, vmem(coarse),
    )
    got = vmem(swap_cores(sent))
    return call(
        output_kernel, "output", [((1,) + FIELD, F32)] * 2, vmem(end), residual, got, place,
        keep=False,
    )


def solution(mesh):
    slices, depth = mesh.devices.shape
    count = slices // 2
    pairs = Mesh(mesh.devices.reshape(count, 2, depth), ("q", "c", "space"))
    tm = ("q", "c")
    return jax.shard_map(
        functools.partial(body, count, depth),
        mesh=pairs,
        in_specs=(
            P(None, "space"),
            P(tm, None, "space"),
            P(tm, None, "space"),
            P(None, None, "space"),
            P(),
            P(None, "space"),
            P(None, "space"),
        ),
        out_specs=(P(tm, None, "space"), P(tm, None, "space")),
        check_vma=False,
    )
```

```python
import functools

import jax
import jax.numpy as jnp
from jax import lax
from jax.experimental import pallas as pl
from jax.experimental.pallas import tpu as pltpu
from jax.sharding import Mesh, PartitionSpec as P


VALUES = 64
LANES = 128
HALF = 64
STEPS = 4
STAGES = 2 * STEPS
HIGHEST = lax.Precision.HIGHEST
F32 = jnp.float32
FIELD = (VALUES, LANES)


def vmem(x):
    return pltpu.with_memory_space_constraint(x, pltpu.VMEM)


def hbm(x):
    return pltpu.with_memory_space_constraint(x, pltpu.HBM)


def call(kernel, name, outs, *args, keep=True, fetch=False, scratch=(FIELD,), flops=1 << 22):
    whole = pl.BlockSpec(memory_space=pltpu.VMEM)
    shapes = tuple(
        pltpu.VMEM(shape, dtype) if keep else jax.ShapeDtypeStruct(shape, dtype)
        for shape, dtype in outs
    )
    held = [pltpu.VMEM(shape, F32) for shape in scratch]
    if fetch:
        held += [pltpu.VMEM(arg.shape, arg.dtype) for arg in args[:3]]
        held += [pltpu.SemaphoreType.DMA((12,))]
    return pl.pallas_call(
        kernel,
        out_shape=shapes,
        in_specs=[pl.BlockSpec(memory_space=pl.ANY) if fetch else whole] * len(args),
        out_specs=(whole,) * len(shapes),
        scratch_shapes=held,
        cost_estimate=pl.CostEstimate(flops=flops, bytes_accessed=1 << 20, transcendentals=0),
        compiler_params=pltpu.CompilerParams(vmem_limit_bytes=16 << 20),
        name=name,
    )(*args)


def fetched(copies):
    for copy in copies:
        copy.start()
    for copy in copies:
        copy.wait()


def low_half():
    return lax.broadcasted_iota(jnp.int32, FIELD, 1) < HALF


def swap_halves(x):
    return pltpu.roll(x, HALF, 1)


def columns(x, index):
    return jnp.take_along_axis(x, jnp.broadcast_to(index, x.shape), axis=1)


def twice(row):
    return jnp.concatenate([row, row], axis=1)


def layer_rows(send_ref, core):
    lowest, highest = send_ref[0:1, :], send_ref[1:2, :]
    mine = jnp.where(core == 0, lowest, highest)
    other = jnp.where(core == 0, highest, lowest)
    return twice(mine), twice(other)


def apply_inverse(inverse_ref, scratch, vector):
    scratch[...] = vector
    sums = [None, None]
    for j in range(VALUES):
        term = inverse_ref[j] * scratch[j : j + 1, :]
        sums[j % 2] = term if sums[j % 2] is None else sums[j % 2] + term
    return sums[0] + sums[1]


def product(left, right):
    return jnp.dot(left, right, precision=HIGHEST, preferred_element_type=F32)


def own_faces(field, index, valid, faces):
    picked = [
        columns(field, index[f : f + 1, :]) * jnp.broadcast_to(valid[f : f + 1, :], FIELD)
        for f in range(4)
    ]
    return product(faces[:, : 4 * VALUES], jnp.concatenate(picked, axis=0))


def share_kernel(send_any, forcing_any, gain_any, state_any, own_ref, out_ref, start_ref, state_ref,
                 send_ref, forcing_ref, gain_ref, sems):
    core = lax.axis_index("c")
    fetched([
        pltpu.make_async_copy(send_any, send_ref, sems.at[0]),
        pltpu.make_async_copy(forcing_any, forcing_ref, sems.at[1]),
        pltpu.make_async_copy(gain_any, gain_ref, sems.at[2]),
        pltpu.make_async_copy(state_any, state_ref, sems.at[3]),
    ])
    mine, other = layer_rows(send_ref, core)
    low = low_half()
    fields = [forcing_ref[m] for m in range(STEPS)] + [gain_ref[0]]
    for m in range(0, STEPS, 2):
        out_ref[m // 2] = jnp.where(low, columns(fields[m], other), columns(fields[m + 1], other))
    out_ref[STEPS // 2] = columns(fields[STEPS], other)
    for m, field in enumerate(fields):
        own_ref[m] = columns(field, mine)
    start_ref[...] = columns(state_ref[...], mine)


def tables_kernel(
    send_any, neighbor_any, blocks_any, inverse_any, index_ref, valid_ref, place_ref, faces_ref,
    table_ref, chunks_ref, send_ref, neighbor_ref, blocks_ref, sems
):
    core = lax.axis_index("c")
    group = VALUES // 8
    small = [
        pltpu.make_async_copy(send_any, send_ref, sems.at[8]),
        pltpu.make_async_copy(neighbor_any, neighbor_ref, sems.at[9]),
        pltpu.make_async_copy(blocks_any, blocks_ref, sems.at[10]),
    ]
    large = [
        pltpu.make_async_copy(
            inverse_any.at[:, pl.ds(8 * k, 8), :], chunks_ref.at[k], sems.at[k]
        )
        for k in range(group)
    ]
    for copy in small + large:
        copy.start()
    for copy in small:
        copy.wait()
    mine, _other = layer_rows(send_ref, core)
    order = jnp.concatenate([send_ref[0:1, :], send_ref[1:2, :]], axis=1)
    down = jnp.transpose(jnp.broadcast_to(order.astype(F32), (LANES, LANES)))
    across = lax.broadcasted_iota(jnp.int32, (LANES, LANES), 1).astype(F32)
    at = lax.broadcasted_iota(jnp.int32, (LANES, LANES), 0).astype(F32)
    place = jnp.sum(jnp.where(down == across, at, 0.0), axis=0, keepdims=True).astype(jnp.int32)
    place = jnp.broadcast_to(place, (8, LANES))
    place_ref[...] = place
    pad = jnp.zeros((2, LANES), jnp.int32)
    local = columns(jnp.concatenate([neighbor_ref[...], pad], axis=0), mine)
    valid_ref[...] = (local >= 0).astype(F32)
    lane = lax.broadcasted_iota(jnp.int32, (8, LANES), 1)
    spot = columns(place, jnp.clip(local, 0, LANES - 1))
    index_ref[...] = jnp.bitwise_and(spot, HALF - 1) + jnp.where(lane < HALF, 0, HALF)
    for f in range(4):
        faces_ref[:, f * VALUES : (f + 1) * VALUES] = blocks_ref[f]
    faces_ref[:, 4 * VALUES : 5 * VALUES] = jnp.where(core == 0, blocks_ref[4], blocks_ref[5])
    faces_ref[:, 5 * VALUES : 6 * VALUES] = jnp.where(core == 0, blocks_ref[5], blocks_ref[4])
    for k in range(group):
        large[k].wait()
        for j in range(8):
            table_ref[8 * k + j] = columns(chunks_ref[k, :, j, :], mine)


def first_kernel(
    own_ref, got_ref, start_ref, index_ref, valid_ref, faces_ref, table_ref, sources_ref, gain_ref,
    pair_ref, right_ref, ahead_ref, scratch
):
    core = lax.axis_index("c")
    low = low_half()
    is_own = low == (core == 0)
    for m in range(STEPS + 1):
        got = got_ref[m // 2]
        turned = swap_halves(got)
        if m % 2 == 0:
            other = jnp.where(core == 0, turned, got)
        else:
            other = jnp.where(core == 0, got, turned)
        value = jnp.where(is_own, own_ref[m], other)
        if m < STEPS:
            sources_ref[m] = value
        else:
            gain_ref[...] = value
    first = jnp.logical_and(low, lax.axis_index("q") == 0)
    right = jnp.where(first, start_ref[...], 0.0) + sources_ref[0]
    right_ref[...] = right
    pair_ref[0] = jnp.zeros(FIELD, F32)
    field = apply_inverse(table_ref, scratch, right)
    pair_ref[1] = field
    ahead_ref[...] = own_faces(field, index_ref[...], valid_ref[...], faces_ref[...])


def advance(plan, refs, sourced, scratch):
    (pair_ref, right_ref, ahead_ref, near_ref, far_ref, index_ref, valid_ref, faces_ref, table_ref,
     sources_ref, pair_out, right_out, ahead_out) = refs
    active, stages = plan
    core = lax.axis_index("c")

    @pl.when(core == active)
    def _run():
        index, valid, faces = index_ref[...], valid_ref[...], faces_ref[...]
        layers = [
            jnp.concatenate([ref[slot] for _, slot in stages], axis=1) for ref in (far_ref, near_ref)
        ]
        across = product(faces[:, 4 * VALUES :], jnp.concatenate(layers, axis=0))
        field = pair_ref[1]
        right = right_ref[...]
        summed = ahead_ref[...]
        for place, (stage, _) in enumerate(stages):
            pair_out[0] = field
            if place > 0:
                summed = own_faces(field, index, valid, faces)
            summed = summed + across[:, place * LANES : (place + 1) * LANES]
            field = apply_inverse(table_ref, scratch, right - summed)
            if stage % 2 == 1 and stage < STAGES - 1:
                right = field
                if sourced:
                    right = right + sources_ref[(stage + 1) // 2]
                field = apply_inverse(table_ref, scratch, right)
        pair_out[1] = field
        right_out[...] = right

    @pl.when(core != active)
    def _keep():
        pair_out[...] = pair_ref[...]
        right_out[...] = right_ref[...]
        ahead_out[...] = own_faces(pair_ref[1], index_ref[...], valid_ref[...], faces_ref[...])


def advance_kernel(plan, sourced, *refs):
    advance(plan, refs[:-1], sourced, refs[-1])


def ends_kernel(plan, count, *refs):
    (*inner, gain_ref, pair_out, chunk_ref, scratch, right_out, ahead_out) = refs
    advance(plan, (*inner, pair_out, right_out, ahead_out), True, scratch)
    low = low_half()
    gain, end = gain_ref[...], pair_out[1]
    summed = gain * swap_halves(end) + end
    chunk = jnp.where(low, gain * swap_halves(gain), summed)
    for q in range(count):
        chunk_ref[q] = chunk


def ends_last_kernel(plan, count, *refs):
    (*inner, gain_ref, shift_ref, pair_out, residual_ref, chunk_ref, scratch, right_out, ahead_out) = refs
    advance(plan, (*inner, pair_out, right_out, ahead_out), False, scratch)
    gain = gain_ref[...]
    residual = pair_out[1] - gain * shift_ref[...]
    residual_ref[...] = residual
    summed = gain * swap_halves(residual) + residual
    low = low_half()[:HALF // 2]
    chunk = jnp.where(low, swap_halves(summed)[: VALUES // 2], summed[VALUES // 2 :])
    for q in range(count):
        chunk_ref[q] = chunk


def chained(count, before, gain, residual):
    before = jnp.where(low_half(), swap_halves(before), before)
    return jnp.where(low_half(), before, swap_halves(gain * before + residual))


def restart_kernel(
    count, all_ref, end_ref, gain_ref, index_ref, valid_ref, faces_ref, table_ref, shift_ref,
    coarse_ref, pair_ref, ahead_ref, scratch
):
    mine = lax.axis_index("q")
    before = jnp.zeros(FIELD, F32)
    for q in range(count):
        chunk = all_ref[q]
        before = jnp.where(q < mine, swap_halves(chunk) * before + chunk, before)
    gain, end = gain_ref[...], end_ref[1]
    shift = chained(count, before, gain, end)
    shift_ref[...] = shift
    coarse_ref[...] = gain * shift + end
    pair_ref[0] = jnp.zeros(FIELD, F32)
    field = apply_inverse(table_ref, scratch, shift)
    pair_ref[1] = field
    ahead_ref[...] = own_faces(field, index_ref[...], valid_ref[...], faces_ref[...])


def finish_kernel(count, all_ref, gains_ref, residual_ref, gain_ref, coarse_ref, end_ref, out_ref, _):
    core = lax.axis_index("c")
    mine = lax.axis_index("q")
    low = low_half()
    before = jnp.zeros(FIELD, F32)
    for q in range(count):
        chunk = all_ref[q]
        summed = jnp.concatenate([swap_halves(chunk), chunk], axis=0)
        before = jnp.where(q < mine, swap_halves(gains_ref[q]) * before + summed, before)
    gain, residual = gain_ref[...], residual_ref[...]
    shift = chained(count, before, gain, residual)
    end = coarse_ref[...] + (gain * shift + residual)
    end_ref[...] = end
    out_ref[...] = jnp.where(
        core == 0,
        jnp.where(low, swap_halves(end), residual),
        jnp.where(low, end, swap_halves(residual)),
    )


def output_kernel(end_ref, residual_ref, got_ref, place_ref, end_out, residual_out, _):
    core = lax.axis_index("c")
    low = low_half()
    got = got_ref[...]
    turned = swap_halves(got)
    end, residual = end_ref[...], residual_ref[...]
    end = jnp.where(core == 0, jnp.where(low, end, turned), jnp.where(low, got, end))
    residual = jnp.where(
        core == 0, jnp.where(low, residual, got), jnp.where(low, turned, residual)
    )
    place = place_ref[0:1, :]
    end_out[0] = columns(end, place)
    residual_out[0] = columns(residual, place)


def plans():
    yield 1, [(0, 1)]
    for half in range(2, STAGES + 1):
        yield half % 2, [(half - 2, 0), (half - 1, 1)]
    yield (STAGES + 1) % 2, [(STAGES - 1, 0)]


def body(count, depth, initial_state, forcing, coarse_gain, block_inverse, face_blocks, neighbor, send_rows):
    def swap_cores(x):
        return lax.ppermute(x, "c", [(0, 1), (1, 0)])

    def halo(x, to):
        if to == 1:
            across = [(z + 1, depth + z) for z in range(depth - 1)]
        else:
            across = [(depth + z, z + 1) for z in range(depth - 1)]
        far = lax.ppermute(x, ("c", "space"), across)
        near = lax.ppermute(x, "c", [(1 - to, to)])
        return vmem(near), vmem(far)

    field, pair_shape = (FIELD, F32), ((2,) + FIELD, F32)
    own, sent, start = call(
        share_kernel, "share",
        [((STEPS + 1,) + FIELD, F32), ((STEPS // 2 + 1,) + FIELD, F32), field],
        hbm(send_rows), hbm(forcing), hbm(coarse_gain), hbm(initial_state), fetch=True,
    )
    got = swap_cores(sent)
    index, valid, place, faces, table = call(
        tables_kernel, "tables",
        [((8, LANES), jnp.int32), ((8, LANES), F32), ((8, LANES), jnp.int32),
         ((VALUES, 6 * VALUES), F32), ((VALUES,) + FIELD, F32)],
        hbm(send_rows), hbm(neighbor), hbm(face_blocks), hbm(block_inverse), fetch=True,
        scratch=((VALUES // 8, VALUES, 8, LANES),),
    )
    index, valid, place, faces, table = map(vmem, (index, valid, place, faces, table))
    operator = (index, valid, faces, table)
    state = [pair_shape, field, field]
    sources, gain, *now = call(
        first_kernel, "first", [((STEPS,) + FIELD, F32), field, *state],
        vmem(own), vmem(got), vmem(start), *operator,
    )
    sources, gain = vmem(sources), vmem(gain)
    half_phases = list(plans())
    final = half_phases[-1]

    def inner(now, to):
        now = [vmem(x) for x in now]
        return (*now, *halo(now[0], to), *operator, sources)

    for plan in half_phases[:-1]:
        now = call(
            functools.partial(advance_kernel, plan, True), "advance", state, *inner(now, plan[0])
        )
    pair, chunk = call(
        functools.partial(ends_kernel, final, count), "ends",
        [pair_shape, ((count,) + FIELD, F32)], *inner(now, final[0]), gain, scratch=(FIELD,) * 3,
    )
    gathered = vmem(lax.all_to_all(chunk, "q", 0, 0))
    shift, coarse, *now = call(
        functools.partial(restart_kernel, count), "restart", [field, field, pair_shape, field],
        gathered, vmem(pair), gain, *operator,
    )
    shift = vmem(shift)
    now = [now[0], shift, now[1]]
    for plan in half_phases[:-1]:
        now = call(
            functools.partial(advance_kernel, plan, False), "advance", state, *inner(now, plan[0])
        )
    pair, residual, chunk = call(
        functools.partial(ends_last_kernel, final, count), "ends",
        [pair_shape, field, ((count, VALUES // 2, LANES), F32)],
        *inner(now, final[0]), gain, shift, scratch=(FIELD,) * 3,
    )
    sums = vmem(lax.all_to_all(chunk, "q", 0, 0))
    residual = vmem(residual)
    end, sent = call(
        functools.partial(finish_kernel, count), "finish", [field, field],
        sums, gathered, residual, gain, vmem(coarse),
    )
    got = vmem(swap_cores(sent))
    return call(
        output_kernel, "output", [((1,) + FIELD, F32)] * 2, vmem(end), residual, got, place,
        keep=False,
    )


def solution(mesh):
    slices, depth = mesh.devices.shape
    count = slices // 2
    pairs = Mesh(mesh.devices.reshape(count, 2, depth), ("q", "c", "space"))
    tm = ("q", "c")
    return jax.shard_map(
        functools.partial(body, count, depth),
        mesh=pairs,
        in_specs=(
            P(None, "space"),
            P(tm, None, "space"),
            P(tm, None, "space"),
            P(None, None, "space"),
            P(),
            P(None, "space"),
            P(None, "space"),
        ),
        out_specs=(P(tm, None, "space"), P(tm, None, "space")),
        check_vma=False,
    )
```

```python
import functools

import jax
import jax.numpy as jnp
from jax import lax
from jax.experimental import pallas as pl
from jax.experimental.pallas import tpu as pltpu
from jax.sharding import Mesh, PartitionSpec as P


VALUES = 64
LANES = 128
HALF = 64
STEPS = 4
STAGES = 2 * STEPS
HIGHEST = lax.Precision.HIGHEST
F32 = jnp.float32
FIELD = (VALUES, LANES)


def vmem(x):
    return pltpu.with_memory_space_constraint(x, pltpu.VMEM)


def hbm(x):
    return pltpu.with_memory_space_constraint(x, pltpu.HBM)


def call(kernel, name, outs, *args, keep=True, fetch=False, scratch=(FIELD,), flops=1 << 22):
    whole = pl.BlockSpec(memory_space=pltpu.VMEM)
    shapes = tuple(
        pltpu.VMEM(shape, dtype) if keep else jax.ShapeDtypeStruct(shape, dtype)
        for shape, dtype in outs
    )
    held = [pltpu.VMEM(shape, F32) for shape in scratch]
    if fetch:
        held += [pltpu.SemaphoreType.DMA((16,))]
    return pl.pallas_call(
        kernel,
        out_shape=shapes,
        in_specs=[pl.BlockSpec(memory_space=pl.ANY) if fetch else whole] * len(args),
        out_specs=(whole,) * len(shapes),
        scratch_shapes=held,
        cost_estimate=pl.CostEstimate(flops=flops, bytes_accessed=1 << 20, transcendentals=0),
        compiler_params=pltpu.CompilerParams(vmem_limit_bytes=16 << 20),
        name=name,
    )(*args)


def low_half():
    return lax.broadcasted_iota(jnp.int32, FIELD, 1) < HALF


def swap_halves(x):
    return pltpu.roll(x, HALF, 1)


def columns(x, index):
    return jnp.take_along_axis(x, jnp.broadcast_to(index, x.shape), axis=1)


def twice(row):
    return jnp.concatenate([row, row], axis=1)


def layer_rows(send_ref, core):
    lowest, highest = send_ref[0:1, :], send_ref[1:2, :]
    mine = jnp.where(core == 0, lowest, highest)
    other = jnp.where(core == 0, highest, lowest)
    return twice(mine), twice(other)


def apply_inverse(inverse_ref, scratch, vector):
    scratch[...] = vector
    sums = [None, None]
    for j in range(VALUES):
        term = inverse_ref[j] * scratch[j : j + 1, :]
        sums[j % 2] = term if sums[j % 2] is None else sums[j % 2] + term
    return sums[0] + sums[1]


def product(left, right):
    return jnp.dot(left, right, precision=HIGHEST, preferred_element_type=F32)


def own_faces(field, index, valid, faces):
    picked = [
        columns(field, index[f : f + 1, :]) * jnp.broadcast_to(valid[f : f + 1, :], FIELD)
        for f in range(4)
    ]
    return product(faces[:, : 4 * VALUES], jnp.concatenate(picked, axis=0))


def share_kernel(send_any, forcing_any, gain_any, state_any, neighbor_any, blocks_any, inverse_any,
                 own_ref, out_ref, start_ref, send_ref, neighbor_ref, blocks_ref, inverse_ref,
                 state_ref, forcing_ref, gain_ref, sems):
    core = lax.axis_index("c")
    part = VALUES // 8
    first = [
        pltpu.make_async_copy(send_any, send_ref, sems.at[0]),
        pltpu.make_async_copy(forcing_any, forcing_ref, sems.at[1]),
        pltpu.make_async_copy(gain_any, gain_ref, sems.at[2]),
        pltpu.make_async_copy(state_any, state_ref, sems.at[3]),
    ]
    later = [
        pltpu.make_async_copy(neighbor_any, neighbor_ref, sems.at[4]),
        pltpu.make_async_copy(blocks_any, blocks_ref, sems.at[5]),
    ] + [
        pltpu.make_async_copy(
            inverse_any.at[pl.ds(part * k, part)], inverse_ref.at[pl.ds(part * k, part)],
            sems.at[8 + k],
        )
        for k in range(8)
    ]
    for copy in first + later:
        copy.start()
    for copy in first:
        copy.wait()
    mine, other = layer_rows(send_ref, core)
    low = low_half()
    fields = [forcing_ref[m] for m in range(STEPS)] + [gain_ref[0]]
    for m in range(0, STEPS, 2):
        out_ref[m // 2] = jnp.where(low, columns(fields[m], other), columns(fields[m + 1], other))
    out_ref[STEPS // 2] = columns(fields[STEPS], other)
    for m, field in enumerate(fields):
        own_ref[m] = columns(field, mine)
    start_ref[...] = columns(state_ref[...], mine)
    for copy in later:
        copy.wait()


def tables_kernel(
    send_ref, neighbor_ref, blocks_ref, inverse_ref, index_ref, valid_ref, place_ref, faces_ref,
    table_ref, _
):
    core = lax.axis_index("c")
    mine, _other = layer_rows(send_ref, core)
    order = jnp.concatenate([send_ref[0:1, :], send_ref[1:2, :]], axis=1)
    down = jnp.transpose(jnp.broadcast_to(order.astype(F32), (LANES, LANES)))
    across = lax.broadcasted_iota(jnp.int32, (LANES, LANES), 1).astype(F32)
    at = lax.broadcasted_iota(jnp.int32, (LANES, LANES), 0).astype(F32)
    place = jnp.sum(jnp.where(down == across, at, 0.0), axis=0, keepdims=True).astype(jnp.int32)
    place = jnp.broadcast_to(place, (8, LANES))
    place_ref[...] = place
    pad = jnp.zeros((2, LANES), jnp.int32)
    local = columns(jnp.concatenate([neighbor_ref[...], pad], axis=0), mine)
    valid_ref[...] = (local >= 0).astype(F32)
    lane = lax.broadcasted_iota(jnp.int32, (8, LANES), 1)
    spot = columns(place, jnp.clip(local, 0, LANES - 1))
    index_ref[...] = jnp.bitwise_and(spot, HALF - 1) + jnp.where(lane < HALF, 0, HALF)
    for f in range(4):
        faces_ref[:, f * VALUES : (f + 1) * VALUES] = blocks_ref[f]
    faces_ref[:, 4 * VALUES : 5 * VALUES] = jnp.where(core == 0, blocks_ref[4], blocks_ref[5])
    faces_ref[:, 5 * VALUES : 6 * VALUES] = jnp.where(core == 0, blocks_ref[5], blocks_ref[4])
    for j in range(VALUES):
        table_ref[j] = columns(inverse_ref[:, j, :], mine)


def packed(x):
    rows = VALUES // 2
    return jnp.where(low_half()[:rows], x[:rows], swap_halves(x)[rows:])


def unpacked(x):
    low, turned = low_half()[: VALUES // 2], swap_halves(x)
    return jnp.concatenate([jnp.where(low, x, turned), jnp.where(low, turned, x)], axis=0)


def first_kernel(
    own_ref, got_ref, start_ref, table_ref, sources_ref, gain_ref, pair_ref, right_ref, scratch
):
    core = lax.axis_index("c")
    low = low_half()
    is_own = low == (core == 0)
    for m in range(STEPS + 1):
        got = got_ref[m // 2]
        turned = swap_halves(got)
        if m % 2 == 0:
            other = jnp.where(core == 0, turned, got)
        else:
            other = jnp.where(core == 0, got, turned)
        value = jnp.where(is_own, own_ref[m], other)
        if m < STEPS:
            sources_ref[m] = value
        else:
            gain_ref[...] = value
    first = jnp.logical_and(low, lax.axis_index("q") == 0)
    right = jnp.where(first, start_ref[...], 0.0) + sources_ref[0]
    right_ref[...] = right
    begin(right, table_ref, pair_ref, scratch)


def begin(right, table_ref, pair_ref, scratch):
    @pl.when(lax.axis_index("c") == 0)
    def _field():
        pair_ref[0] = jnp.zeros(FIELD, F32)
        pair_ref[1] = apply_inverse(table_ref, scratch, right)

    @pl.when(lax.axis_index("c") != 0)
    def _later():
        pair_ref[...] = jnp.zeros((2,) + FIELD, F32)


def late_kernel(pair_ref, right_ref, index_ref, valid_ref, faces_ref, table_ref, pair_out, ahead_ref,
                scratch):
    core = lax.axis_index("c")

    @pl.when(core == 1)
    def _run():
        field = apply_inverse(table_ref, scratch, right_ref[...])
        pair_out[0] = pair_ref[0]
        pair_out[1] = field
        ahead_ref[...] = own_faces(field, index_ref[...], valid_ref[...], faces_ref[...])

    @pl.when(core == 0)
    def _keep():
        pair_out[...] = pair_ref[...]


def ahead_kernel(active, pair_ref, index_ref, valid_ref, faces_ref, ahead_ref, _):
    @pl.when(lax.axis_index("c") == active)
    def _run():
        ahead_ref[...] = own_faces(pair_ref[1], index_ref[...], valid_ref[...], faces_ref[...])


def advance(plan, refs, sourced, scratch):
    (pair_ref, right_ref, ahead_ref, near_ref, far_ref, index_ref, valid_ref, faces_ref, table_ref,
     sources_ref, pair_out, right_out) = refs
    active, stages = plan
    core = lax.axis_index("c")

    @pl.when(core == active)
    def _run():
        index, valid, faces = index_ref[...], valid_ref[...], faces_ref[...]
        layers = [
            jnp.concatenate([ref[slot] for _, slot in stages], axis=1) for ref in (far_ref, near_ref)
        ]
        across = product(faces[:, 4 * VALUES :], jnp.concatenate(layers, axis=0))
        field = pair_ref[1]
        right = right_ref[...]
        summed = ahead_ref[...]
        for place, (stage, _) in enumerate(stages):
            pair_out[0] = field
            if place > 0:
                summed = own_faces(field, index, valid, faces)
            summed = summed + across[:, place * LANES : (place + 1) * LANES]
            field = apply_inverse(table_ref, scratch, right - summed)
            if stage % 2 == 1 and stage < STAGES - 1:
                right = field
                if sourced:
                    right = right + sources_ref[(stage + 1) // 2]
                field = apply_inverse(table_ref, scratch, right)
        pair_out[1] = field
        right_out[...] = right

    @pl.when(core != active)
    def _keep():
        pair_out[...] = pair_ref[...]
        right_out[...] = right_ref[...]


def advance_kernel(plan, sourced, *refs):
    advance(plan, refs[:-1], sourced, refs[-1])


def ends_kernel(plan, sourced, count, *refs):
    if sourced:
        (*inner, gain_ref, residual_ref, chunk_ref, scratch, pair_out, right_out) = refs
    else:
        (*inner, gain_ref, shift_ref, residual_ref, chunk_ref, scratch, pair_out, right_out) = refs
    advance(plan, (*inner, pair_out, right_out), sourced, scratch)
    gain = gain_ref[...]
    residual = pair_out[1]
    if not sourced:
        residual = residual - gain * shift_ref[...]
    residual_ref[...] = residual
    rows = VALUES // 2
    chunk = packed(swap_halves(gain * swap_halves(residual) + residual))
    if sourced:
        gains = packed(gain * swap_halves(gain))
    for q in range(count):
        chunk_ref[q, :rows] = chunk
        if sourced:
            chunk_ref[q, rows:] = gains


def scanned(count, sums_ref, gains_ref):
    mine = lax.axis_index("q")
    rows = VALUES // 2
    before = jnp.zeros((rows, LANES), F32)
    for q in range(count):
        after = gains_ref[q, rows:] * before + sums_ref[q, :rows]
        before = jnp.where(q < mine, after, before)
    return unpacked(before)


def shifted(before, gain, residual):
    return jnp.where(low_half(), before, swap_halves(gain * before + residual))


def restart_kernel(
    count, sums_ref, end_ref, gain_ref, table_ref, shift_ref, coarse_ref, pair_ref,
    scratch
):
    gain, end = gain_ref[...], end_ref[...]
    shift = shifted(scanned(count, sums_ref, sums_ref), gain, end)
    shift_ref[...] = shift
    coarse_ref[...] = gain * shift + end
    begin(shift, table_ref, pair_ref, scratch)


def finish_kernel(count, sums_ref, gains_ref, residual_ref, gain_ref, coarse_ref, end_ref, out_ref, _):
    core = lax.axis_index("c")
    low = low_half()
    gain, residual = gain_ref[...], residual_ref[...]
    shift = shifted(scanned(count, sums_ref, gains_ref), gain, residual)
    end = coarse_ref[...] + (gain * shift + residual)
    end_ref[...] = end
    out_ref[...] = jnp.where(
        core == 0,
        jnp.where(low, swap_halves(end), residual),
        jnp.where(low, end, swap_halves(residual)),
    )


def output_kernel(end_ref, residual_ref, got_ref, place_ref, end_out, residual_out, _):
    core = lax.axis_index("c")
    low = low_half()
    got = got_ref[...]
    turned = swap_halves(got)
    end, residual = end_ref[...], residual_ref[...]
    end = jnp.where(core == 0, jnp.where(low, end, turned), jnp.where(low, got, end))
    residual = jnp.where(
        core == 0, jnp.where(low, residual, got), jnp.where(low, turned, residual)
    )
    place = place_ref[0:1, :]
    end_out[0] = columns(end, place)
    residual_out[0] = columns(residual, place)


def plans():
    yield 1, [(0, 1)]
    for half in range(2, STAGES + 1):
        yield half % 2, [(half - 2, 0), (half - 1, 1)]
    yield (STAGES + 1) % 2, [(STAGES - 1, 0)]


def body(count, depth, initial_state, forcing, coarse_gain, block_inverse, face_blocks, neighbor, send_rows):
    def swap_cores(x):
        return lax.ppermute(x, "c", [(0, 1), (1, 0)])

    def halo(x, to):
        if to == 1:
            across = [(z + 1, depth + z) for z in range(depth - 1)]
        else:
            across = [(depth + z, z + 1) for z in range(depth - 1)]
        far = lax.ppermute(x, ("c", "space"), across)
        near = lax.ppermute(x, "c", [(1 - to, to)])
        return vmem(near), vmem(far)

    field, pair_shape = (FIELD, F32), ((2,) + FIELD, F32)
    raw = (send_rows, neighbor, face_blocks, block_inverse)
    own, sent, start, *raw = call(
        share_kernel, "share",
        [((STEPS + 1,) + FIELD, F32), ((STEPS // 2 + 1,) + FIELD, F32), field,
         *((x.shape, x.dtype) for x in raw)],
        *map(hbm, (send_rows, forcing, coarse_gain, initial_state, *raw[1:])), fetch=True,
        scratch=(FIELD, forcing.shape, coarse_gain.shape),
    )
    got = swap_cores(sent)
    index, valid, place, faces, table = call(
        tables_kernel, "tables",
        [((8, LANES), jnp.int32), ((8, LANES), F32), ((8, LANES), jnp.int32),
         ((VALUES, 6 * VALUES), F32), ((VALUES,) + FIELD, F32)],
        *map(vmem, raw),
    )
    index, valid, place, faces, table = map(vmem, (index, valid, place, faces, table))
    sources, gain, pair, right = call(
        first_kernel, "first", [((STEPS,) + FIELD, F32), field, pair_shape, field],
        vmem(own), vmem(got), vmem(start), table,
    )
    sources, gain = vmem(sources), vmem(gain)
    half_phases = list(plans())

    def evolve(pair, right, sourced, shift):
        for number, plan in enumerate(half_phases):
            pair, right = vmem(pair), vmem(right)
            near, far = halo(pair, plan[0])
            if number == 0:
                pair, ahead = call(
                    late_kernel, "late", [pair_shape, field], pair, right, index, valid, faces, table
                )
            else:
                (ahead,) = call(
                    functools.partial(ahead_kernel, plan[0]), "ahead", [field], pair, index, valid,
                    faces,
                )
            args = (vmem(pair), right, vmem(ahead), near, far, index, valid, faces, table, sources)
            if number < len(half_phases) - 1:
                pair, right = call(
                    functools.partial(advance_kernel, plan, sourced), "advance",
                    [pair_shape, field], *args,
                )
        residual, chunk = call(
            functools.partial(ends_kernel, plan, sourced, count), "ends",
            [field, ((count, VALUES if sourced else VALUES // 2, LANES), F32)], *args, gain,
            *shift, scratch=(FIELD, (2,) + FIELD, FIELD),
        )
        return vmem(residual), vmem(lax.all_to_all(chunk, "q", 0, 0))

    end, sums = evolve(pair, right, True, ())
    shift, coarse, pair = call(
        functools.partial(restart_kernel, count), "restart", [field, field, pair_shape],
        sums, end, gain, table,
    )
    shift = vmem(shift)
    gains = sums
    residual, sums = evolve(pair, shift, False, (shift,))
    end, sent = call(
        functools.partial(finish_kernel, count), "finish", [field, field],
        sums, gains, residual, gain, vmem(coarse),
    )
    got = vmem(swap_cores(sent))
    return call(
        output_kernel, "output", [((1,) + FIELD, F32)] * 2, vmem(end), residual, got, place,
        keep=False,
    )


def solution(mesh):
    slices, depth = mesh.devices.shape
    count = slices // 2
    pairs = Mesh(mesh.devices.reshape(count, 2, depth), ("q", "c", "space"))
    tm = ("q", "c")
    return jax.shard_map(
        functools.partial(body, count, depth),
        mesh=pairs,
        in_specs=(
            P(None, "space"),
            P(tm, None, "space"),
            P(tm, None, "space"),
            P(None, None, "space"),
            P(),
            P(None, "space"),
            P(None, "space"),
        ),
        out_specs=(P(tm, None, "space"), P(tm, None, "space")),
        check_vma=False,
    )
```

```python
import functools

import jax
import jax.numpy as jnp
from jax import lax
from jax.experimental import pallas as pl
from jax.experimental.pallas import tpu as pltpu
from jax.sharding import Mesh, PartitionSpec as P


VALUES = 64
LANES = 128
HALF = 64
STEPS = 4
STAGES = 2 * STEPS
F32 = jnp.float32
BF16 = jnp.bfloat16
FIELD = (VALUES, LANES)


def vmem(x):
    return pltpu.with_memory_space_constraint(x, pltpu.VMEM)


def hbm(x):
    return pltpu.with_memory_space_constraint(x, pltpu.HBM)


def call(kernel, name, outs, *args, keep=True, fetch=False, scratch=(FIELD,), flops=1 << 22):
    whole = pl.BlockSpec(memory_space=pltpu.VMEM)
    shapes = tuple(
        pltpu.VMEM(shape, dtype) if keep else jax.ShapeDtypeStruct(shape, dtype)
        for shape, dtype in outs
    )
    held = [pltpu.VMEM(shape, F32) for shape in scratch]
    if fetch:
        held += [pltpu.SemaphoreType.DMA((16,))]
    return pl.pallas_call(
        kernel,
        out_shape=shapes,
        in_specs=[pl.BlockSpec(memory_space=pl.ANY) if fetch else whole] * len(args),
        out_specs=(whole,) * len(shapes),
        scratch_shapes=held,
        cost_estimate=pl.CostEstimate(flops=flops, bytes_accessed=1 << 20, transcendentals=0),
        compiler_params=pltpu.CompilerParams(vmem_limit_bytes=16 << 20),
        name=name,
    )(*args)


def low_half():
    return lax.broadcasted_iota(jnp.int32, FIELD, 1) < HALF


def swap_halves(x):
    return pltpu.roll(x, HALF, 1)


def columns(x, index):
    return jnp.take_along_axis(x, jnp.broadcast_to(index, x.shape), axis=1)


def twice(row):
    return jnp.concatenate([row, row], axis=1)


def layer_rows(send_ref, core):
    lowest, highest = send_ref[0:1, :], send_ref[1:2, :]
    mine = jnp.where(core == 0, lowest, highest)
    other = jnp.where(core == 0, highest, lowest)
    return twice(mine), twice(other)


def apply_inverse(inverse_ref, scratch, vector):
    scratch[...] = vector
    sums = [None, None]
    for j in range(VALUES):
        term = inverse_ref[j] * scratch[j : j + 1, :]
        sums[j % 2] = term if sums[j % 2] is None else sums[j % 2] + term
    return sums[0] + sums[1]


def halves(x):
    high = x.astype(BF16)
    return high, (x - high.astype(F32)).astype(BF16)


def product(faces, layers):
    width = layers.shape[1]
    parts = jnp.dot(faces, jnp.concatenate(halves(layers), axis=1), preferred_element_type=F32)
    upper, lower = parts[:VALUES], parts[VALUES:]
    return upper[:, :width] + ((upper[:, width:] + lower[:, :width]) + lower[:, width:])


def own_faces(field, index, valid, faces):
    picked = [
        columns(field, index[f : f + 1, :]) * jnp.broadcast_to(valid[f : f + 1, :], FIELD)
        for f in range(4)
    ]
    return product(faces[:, : 4 * VALUES], jnp.concatenate(picked, axis=0))


def share_kernel(send_any, forcing_any, gain_any, state_any, neighbor_any, blocks_any, inverse_any,
                 own_ref, out_ref, start_ref, send_ref, neighbor_ref, blocks_ref, inverse_ref,
                 state_ref, forcing_ref, gain_ref, sems):
    core = lax.axis_index("c")
    part = VALUES // 8
    first = [
        pltpu.make_async_copy(send_any, send_ref, sems.at[0]),
        pltpu.make_async_copy(forcing_any, forcing_ref, sems.at[1]),
        pltpu.make_async_copy(gain_any, gain_ref, sems.at[2]),
        pltpu.make_async_copy(state_any, state_ref, sems.at[3]),
    ]
    later = [
        pltpu.make_async_copy(neighbor_any, neighbor_ref, sems.at[4]),
        pltpu.make_async_copy(blocks_any, blocks_ref, sems.at[5]),
    ] + [
        pltpu.make_async_copy(
            inverse_any.at[pl.ds(part * k, part)], inverse_ref.at[pl.ds(part * k, part)],
            sems.at[8 + k],
        )
        for k in range(8)
    ]
    for copy in first + later:
        copy.start()
    for copy in first:
        copy.wait()
    mine, other = layer_rows(send_ref, core)
    low = low_half()
    fields = [forcing_ref[m] for m in range(STEPS)] + [gain_ref[0]]
    for m in range(0, STEPS, 2):
        out_ref[m // 2] = jnp.where(low, columns(fields[m], other), columns(fields[m + 1], other))
    out_ref[STEPS // 2] = columns(fields[STEPS], other)
    for m, field in enumerate(fields):
        own_ref[m] = columns(field, mine)
    start_ref[...] = columns(state_ref[...], mine)
    for copy in later:
        copy.wait()


def tables_kernel(
    send_ref, neighbor_ref, blocks_ref, inverse_ref, index_ref, valid_ref, place_ref, faces_ref,
    table_ref, _
):
    core = lax.axis_index("c")
    mine, _other = layer_rows(send_ref, core)
    order = jnp.concatenate([send_ref[0:1, :], send_ref[1:2, :]], axis=1)
    down = jnp.transpose(jnp.broadcast_to(order.astype(F32), (LANES, LANES)))
    across = lax.broadcasted_iota(jnp.int32, (LANES, LANES), 1).astype(F32)
    at = lax.broadcasted_iota(jnp.int32, (LANES, LANES), 0).astype(F32)
    place = jnp.sum(jnp.where(down == across, at, 0.0), axis=0, keepdims=True).astype(jnp.int32)
    place = jnp.broadcast_to(place, (8, LANES))
    place_ref[...] = place
    pad = jnp.zeros((2, LANES), jnp.int32)
    local = columns(jnp.concatenate([neighbor_ref[...], pad], axis=0), mine)
    valid_ref[...] = (local >= 0).astype(F32)
    lane = lax.broadcasted_iota(jnp.int32, (8, LANES), 1)
    spot = columns(place, jnp.clip(local, 0, LANES - 1))
    index_ref[...] = jnp.bitwise_and(spot, HALF - 1) + jnp.where(lane < HALF, 0, HALF)
    blocks = [blocks_ref[f] for f in range(4)]
    blocks += [
        jnp.where(core == 0, blocks_ref[4], blocks_ref[5]),
        jnp.where(core == 0, blocks_ref[5], blocks_ref[4]),
    ]
    for f, block in enumerate(blocks):
        high, low = halves(block)
        faces_ref[:VALUES, f * VALUES : (f + 1) * VALUES] = high
        faces_ref[VALUES:, f * VALUES : (f + 1) * VALUES] = low
    for j in range(VALUES):
        table_ref[j] = columns(inverse_ref[:, j, :], mine)


def packed(x):
    rows = VALUES // 2
    return jnp.where(low_half()[:rows], x[:rows], swap_halves(x)[rows:])


def unpacked(x):
    low, turned = low_half()[: VALUES // 2], swap_halves(x)
    return jnp.concatenate([jnp.where(low, x, turned), jnp.where(low, turned, x)], axis=0)


def first_kernel(
    lead, own_ref, got_ref, start_ref, table_ref, sources_ref, gain_ref, field_ref, right_ref, scratch
):
    core = lax.axis_index("c")
    low = low_half()
    is_own = low == (core == 0)
    for m in range(STEPS + 1):
        got = got_ref[m // 2]
        turned = swap_halves(got)
        if m % 2 == 0:
            other = jnp.where(core == 0, turned, got)
        else:
            other = jnp.where(core == 0, got, turned)
        value = jnp.where(is_own, own_ref[m], other)
        if m < STEPS:
            sources_ref[m] = value
        else:
            gain_ref[...] = value
    first = jnp.logical_and(low, lax.axis_index("q") == 0)
    right = jnp.where(first, start_ref[...], 0.0) + sources_ref[0]
    right_ref[...] = right
    begin(lead, right, table_ref, field_ref, scratch)


def begin(lead, right, table_ref, field_ref, scratch):
    @pl.when(lax.axis_index("c") == lead)
    def _field():
        field_ref[...] = apply_inverse(table_ref, scratch, right)

    @pl.when(lax.axis_index("c") != lead)
    def _later():
        field_ref[...] = jnp.zeros(FIELD, F32)


def late_kernel(lead, field_ref, right_ref, index_ref, valid_ref, faces_ref, table_ref, field_out,
                ahead_ref, scratch):
    core = lax.axis_index("c")

    @pl.when(core != lead)
    def _run():
        field = apply_inverse(table_ref, scratch, right_ref[...])
        field_out[...] = field
        ahead_ref[...] = own_faces(field, index_ref[...], valid_ref[...], faces_ref[...])

    @pl.when(core == lead)
    def _keep():
        field_out[...] = field_ref[...]


def ahead_kernel(active, pair_ref, index_ref, valid_ref, faces_ref, ahead_ref, _):
    @pl.when(lax.axis_index("c") == active)
    def _run():
        ahead_ref[...] = own_faces(pair_ref[1], index_ref[...], valid_ref[...], faces_ref[...])


def across_faces(faces, far, near):
    return product(faces[:, 4 * VALUES :], jnp.concatenate([far, near], axis=0))


def open_kernel(lead, field_ref, right_ref, ahead_ref, near_ref, far_ref, faces_ref, table_ref,
                pair_out, scratch):
    core = lax.axis_index("c")

    @pl.when(core != lead)
    def _run():
        summed = ahead_ref[...] + across_faces(faces_ref[...], far_ref[...], near_ref[...])
        pair_out[0] = field_ref[...]
        pair_out[1] = apply_inverse(table_ref, scratch, right_ref[...] - summed)

    @pl.when(core == lead)
    def _keep():
        pair_out[0] = jnp.zeros(FIELD, F32)
        pair_out[1] = field_ref[...]


def advance_kernel(stage, active, sourced, pair_ref, right_ref, ahead_ref, near_ref, far_ref,
                   index_ref, valid_ref, faces_ref, table_ref, sources_ref, pair_out, right_out,
                   scratch):
    core = lax.axis_index("c")

    @pl.when(core == active)
    def _run():
        index, valid, faces = index_ref[...], valid_ref[...], faces_ref[...]
        far, near = (jnp.concatenate([ref[0], ref[1]], axis=1) for ref in (far_ref, near_ref))
        across = across_faces(faces, far, near)
        right = right_ref[...]

        def taken(summed, right, stage):
            field = apply_inverse(table_ref, scratch, right - summed)
            if stage % 2 == 1:
                right = field
                if sourced:
                    right = right + sources_ref[(stage + 1) // 2]
                field = apply_inverse(table_ref, scratch, right)
            return field, right

        field, right = taken(ahead_ref[...] + across[:, :LANES], right, stage)
        pair_out[0] = field
        summed = own_faces(field, index, valid, faces) + across[:, LANES:]
        field, right = taken(summed, right, stage + 1)
        pair_out[1] = field
        right_out[...] = right

    @pl.when(core != active)
    def _keep():
        pair_out[...] = pair_ref[...]
        right_out[...] = right_ref[...]


def last_kernel(lead, pair_ref, right_ref, ahead_ref, near_ref, far_ref, faces_ref, table_ref,
                field_out, scratch):
    core = lax.axis_index("c")

    @pl.when(core == lead)
    def _run():
        summed = ahead_ref[...] + across_faces(faces_ref[...], far_ref[0], near_ref[0])
        field_out[...] = apply_inverse(table_ref, scratch, right_ref[...] - summed)

    @pl.when(core != lead)
    def _keep():
        field_out[...] = pair_ref[1]


def tail_kernel(lead, field_ref, right_ref, near_ref, far_ref, index_ref, valid_ref, faces_ref,
                table_ref, out_ref, scratch):
    core = lax.axis_index("c")
    out_ref[...] = own_faces(field_ref[...], index_ref[...], valid_ref[...], faces_ref[...])

    @pl.when(core == lead)
    def _run():
        summed = out_ref[...] + across_faces(faces_ref[...], far_ref[1], near_ref[1])
        out_ref[...] = apply_inverse(table_ref, scratch, right_ref[...] - summed)


def ends_kernel(lead, sourced, count, *refs):
    if sourced:
        (right_ref, tail_ref, near_ref, far_ref, faces_ref, table_ref, gain_ref, residual_ref,
         chunk_ref, scratch, end_ref) = refs
    else:
        (right_ref, tail_ref, near_ref, far_ref, faces_ref, table_ref, gain_ref, shift_ref,
         residual_ref, chunk_ref, scratch, end_ref) = refs
    core = lax.axis_index("c")

    @pl.when(core != lead)
    def _run():
        summed = tail_ref[...] + across_faces(faces_ref[...], far_ref[...], near_ref[...])
        end_ref[...] = apply_inverse(table_ref, scratch, right_ref[...] - summed)

    @pl.when(core == lead)
    def _keep():
        end_ref[...] = tail_ref[...]

    gain = gain_ref[...]
    residual = end_ref[...]
    if not sourced:
        residual = residual - gain * shift_ref[...]
    residual_ref[...] = residual
    rows = VALUES // 2
    chunk = packed(swap_halves(gain * swap_halves(residual) + residual))
    if sourced:
        gains = packed(gain * swap_halves(gain))
    for q in range(count):
        chunk_ref[q, :rows] = chunk
        if sourced:
            chunk_ref[q, rows:] = gains


def scanned(count, sums_ref, gains_ref):
    mine = lax.axis_index("q")
    rows = VALUES // 2
    before = jnp.zeros((rows, LANES), F32)
    for q in range(count):
        after = gains_ref[q, rows:] * before + sums_ref[q, :rows]
        before = jnp.where(q < mine, after, before)
    return unpacked(before)


def shifted(before, gain, residual):
    return jnp.where(low_half(), before, swap_halves(gain * before + residual))


def restart_kernel(
    lead, count, sums_ref, end_ref, gain_ref, table_ref, shift_ref, coarse_ref, field_ref, scratch
):
    gain, end = gain_ref[...], end_ref[...]
    shift = shifted(scanned(count, sums_ref, sums_ref), gain, end)
    shift_ref[...] = shift
    coarse_ref[...] = gain * shift + end
    begin(lead, shift, table_ref, field_ref, scratch)


def finish_kernel(count, sums_ref, gains_ref, residual_ref, gain_ref, coarse_ref, end_ref, out_ref, _):
    core = lax.axis_index("c")
    low = low_half()
    gain, residual = gain_ref[...], residual_ref[...]
    shift = shifted(scanned(count, sums_ref, gains_ref), gain, residual)
    end = coarse_ref[...] + (gain * shift + residual)
    end_ref[...] = end
    out_ref[...] = jnp.where(
        core == 0,
        jnp.where(low, swap_halves(end), residual),
        jnp.where(low, end, swap_halves(residual)),
    )


def output_kernel(end_ref, residual_ref, got_ref, place_ref, end_out, residual_out, _):
    core = lax.axis_index("c")
    low = low_half()
    got = got_ref[...]
    turned = swap_halves(got)
    end, residual = end_ref[...], residual_ref[...]
    end = jnp.where(core == 0, jnp.where(low, end, turned), jnp.where(low, got, end))
    residual = jnp.where(
        core == 0, jnp.where(low, residual, got), jnp.where(low, turned, residual)
    )
    place = place_ref[0:1, :]
    end_out[0] = columns(end, place)
    residual_out[0] = columns(residual, place)


def body(count, depth, initial_state, forcing, coarse_gain, block_inverse, face_blocks, neighbor, send_rows):
    def swap_cores(x):
        return lax.ppermute(x, "c", [(0, 1), (1, 0)])

    def halo(x, to):
        if to == 1:
            across = [(z + 1, depth + z) for z in range(depth - 1)]
        else:
            across = [(depth + z, z + 1) for z in range(depth - 1)]
        far = lax.ppermute(x, ("c", "space"), across)
        near = lax.ppermute(x, "c", [(1 - to, to)])
        return vmem(near), vmem(far)

    field, pair_shape = (FIELD, F32), ((2,) + FIELD, F32)
    raw = (send_rows, neighbor, face_blocks, block_inverse)
    own, sent, start, *raw = call(
        share_kernel, "share",
        [((STEPS + 1,) + FIELD, F32), ((STEPS // 2 + 1,) + FIELD, F32), field,
         *((x.shape, x.dtype) for x in raw)],
        *map(hbm, (send_rows, forcing, coarse_gain, initial_state, *raw[1:])), fetch=True,
        scratch=(FIELD, forcing.shape, coarse_gain.shape),
    )
    got = swap_cores(sent)
    index, valid, place, faces, table = call(
        tables_kernel, "tables",
        [((8, LANES), jnp.int32), ((8, LANES), F32), ((8, LANES), jnp.int32),
         ((2 * VALUES, 6 * VALUES), BF16), ((VALUES,) + FIELD, F32)],
        *map(vmem, raw),
    )
    index, valid, place, faces, table = map(vmem, (index, valid, place, faces, table))
    operator = (index, valid, faces, table)
    sources, gain, begun, right = call(
        functools.partial(first_kernel, 0), "first", [((STEPS,) + FIELD, F32), field, field, field],
        vmem(own), vmem(got), vmem(start), table,
    )
    sources, gain = vmem(sources), vmem(gain)

    def evolve(lead, now, right, sourced, shift):
        other = 1 - lead
        right = vmem(right)
        now = vmem(now)
        near, far = halo(now, other)
        now, ahead = call(
            functools.partial(late_kernel, lead), "late", [field, field], now, right, *operator
        )
        (pair,) = call(
            functools.partial(open_kernel, lead), "open", [pair_shape],
            vmem(now), right, vmem(ahead), near, far, faces, table,
        )
        for stage in range(STAGES - 1):
            active = (lead, other)[stage % 2]
            pair = vmem(pair)
            near, far = halo(pair, active)
            (ahead,) = call(
                functools.partial(ahead_kernel, active), "ahead", [field], pair, index, valid, faces
            )
            ahead = vmem(ahead)
            if stage < STAGES - 2:
                pair, right = call(
                    functools.partial(advance_kernel, stage, active, sourced), "advance",
                    [pair_shape, field], pair, right, ahead, near, far, *operator, sources,
                )
                right = vmem(right)
        (now,) = call(
            functools.partial(last_kernel, lead), "last", [field],
            pair, right, ahead, near, far, faces, table,
        )
        now = vmem(now)
        tail_halo = near, far
        near, far = halo(now, other)
        (tail,) = call(
            functools.partial(tail_kernel, lead), "tail", [field], now, right, *tail_halo, *operator
        )
        rows = VALUES if sourced else VALUES // 2
        residual, chunk = call(
            functools.partial(ends_kernel, lead, sourced, count), "ends",
            [field, ((count, rows, LANES), F32)],
            right, vmem(tail), near, far, faces, table, gain, *shift, scratch=(FIELD, FIELD),
        )
        return vmem(residual), vmem(lax.all_to_all(chunk, "q", 0, 0))

    end, gains = evolve(0, begun, right, True, ())
    shift, coarse, begun = call(
        functools.partial(restart_kernel, 0, count), "restart", [field, field, field],
        gains, end, gain, table,
    )
    shift = vmem(shift)
    residual, sums = evolve(0, begun, shift, False, (shift,))
    end, sent = call(
        functools.partial(finish_kernel, count), "finish", [field, field],
        sums, gains, residual, gain, vmem(coarse),
    )
    got = vmem(swap_cores(sent))
    return call(
        output_kernel, "output", [((1,) + FIELD, F32)] * 2, vmem(end), residual, got, place,
        keep=False,
    )


def solution(mesh):
    slices, depth = mesh.devices.shape
    count = slices // 2
    pairs = Mesh(mesh.devices.reshape(count, 2, depth), ("q", "c", "space"))
    tm = ("q", "c")
    return jax.shard_map(
        functools.partial(body, count, depth),
        mesh=pairs,
        in_specs=(
            P(None, "space"),
            P(tm, None, "space"),
            P(tm, None, "space"),
            P(None, None, "space"),
            P(),
            P(None, "space"),
            P(None, "space"),
        ),
        out_specs=(P(tm, None, "space"), P(tm, None, "space")),
        check_vma=False,
    )
```

```python
import functools

import jax
import jax.numpy as jnp
from jax import lax
from jax.experimental import pallas as pl
from jax.experimental.pallas import tpu as pltpu
from jax.sharding import Mesh, PartitionSpec as P


VALUES = 64
LANES = 128
HALF = 64
STEPS = 4
STAGES = 2 * STEPS
GX = 8
GY = 8
F32 = jnp.float32
BF16 = jnp.bfloat16
FIELD = (VALUES, LANES)


def vmem(x):
    return pltpu.with_memory_space_constraint(x, pltpu.VMEM)


def hbm(x):
    return pltpu.with_memory_space_constraint(x, pltpu.HBM)


def call(kernel, name, outs, *args, keep=True, fetch=False, scratch=(FIELD,), ints=(), flops=1 << 22):
    whole = pl.BlockSpec(memory_space=pltpu.VMEM)
    shapes = tuple(
        pltpu.VMEM(shape, dtype) if keep else jax.ShapeDtypeStruct(shape, dtype)
        for shape, dtype in outs
    )
    held = [pltpu.VMEM(shape, F32) for shape in scratch]
    held += [pltpu.VMEM(shape, jnp.int32) for shape in ints]
    if fetch:
        held += [pltpu.SemaphoreType.DMA((16,))]
    return pl.pallas_call(
        kernel,
        out_shape=shapes,
        in_specs=[pl.BlockSpec(memory_space=pl.ANY) if fetch else whole] * len(args),
        out_specs=(whole,) * len(shapes),
        scratch_shapes=held,
        cost_estimate=pl.CostEstimate(flops=flops, bytes_accessed=1 << 20, transcendentals=0),
        compiler_params=pltpu.CompilerParams(vmem_limit_bytes=16 << 20),
        name=name,
    )(*args)


def low_half():
    return lax.broadcasted_iota(jnp.int32, FIELD, 1) < HALF


def swap_halves(x):
    return pltpu.roll(x, HALF, 1)


def columns(x, index):
    return jnp.take_along_axis(x, jnp.broadcast_to(index, x.shape), axis=1)


def raster(neighbor):
    ahead = jnp.concatenate([neighbor, jnp.zeros((2, LANES), jnp.int32)], axis=0)
    level = jnp.where(ahead[4:5, :] >= LANES, 0, HALF)
    steps = (ahead >= 0).astype(jnp.int32)
    span = 1
    while span < max(GX, GY):
        on = ahead >= 0
        spot = jnp.clip(ahead, 0, LANES - 1)
        steps = steps + jnp.where(on, jnp.take_along_axis(steps, spot, axis=1), 0)
        ahead = jnp.where(on, jnp.take_along_axis(ahead, spot, axis=1), -1)
        span *= 2
    place = level + GX * steps[2:3, :] + steps[0:1, :]
    down = jnp.transpose(jnp.broadcast_to(place.astype(F32), (LANES, LANES)))
    across = lax.broadcasted_iota(jnp.int32, (LANES, LANES), 1).astype(F32)
    at = lax.broadcasted_iota(jnp.int32, (LANES, LANES), 0).astype(F32)
    order = jnp.sum(jnp.where(down == across, at, 0.0), axis=0, keepdims=True).astype(jnp.int32)
    return jnp.broadcast_to(place, (8, LANES)), jnp.broadcast_to(order, (8, LANES))


def apply_inverse(inverse_ref, scratch, vector):
    scratch[...] = vector
    sums = [None, None]
    for j in range(VALUES):
        term = inverse_ref[j] * scratch[j : j + 1, :]
        sums[j % 2] = term if sums[j % 2] is None else sums[j % 2] + term
    return sums[0] + sums[1]


def halves(x):
    high = x.astype(BF16)
    return high, (x - high.astype(F32)).astype(BF16)


def product(faces, layers):
    width = layers.shape[1]
    parts = jnp.dot(faces, jnp.concatenate(halves(layers), axis=1), preferred_element_type=F32)
    upper, lower = parts[:VALUES], parts[VALUES:]
    return upper[:, :width] + ((upper[:, width:] + lower[:, :width]) + lower[:, width:])


def own_faces(field, faces):
    lane = lax.broadcasted_iota(jnp.int32, FIELD, 1)
    x = jnp.bitwise_and(lane, GX - 1)
    y = jnp.bitwise_and(lane, GX * GY - GX)
    picked = [
        jnp.where(inside, pltpu.roll(field, by % LANES, 1), 0.0)
        for inside, by in ((x > 0, 1), (x < GX - 1, -1), (y > 0, GX), (y < GX * GY - GX, -GX))
    ]
    return product(faces[:, : 4 * VALUES], jnp.concatenate(picked, axis=0))


def share_kernel(neighbor_any, forcing_any, gain_any, state_any, blocks_any, inverse_any,
                 own_ref, out_ref, start_ref, mine_ref, place_ref, blocks_ref, inverse_ref,
                 state_ref, forcing_ref, gain_ref, neighbor_ref, sems):
    core = lax.axis_index("c")
    part = VALUES // 8
    first = [
        pltpu.make_async_copy(neighbor_any, neighbor_ref, sems.at[0]),
        pltpu.make_async_copy(forcing_any, forcing_ref, sems.at[1]),
        pltpu.make_async_copy(gain_any, gain_ref, sems.at[2]),
        pltpu.make_async_copy(state_any, state_ref, sems.at[3]),
    ]
    later = [pltpu.make_async_copy(blocks_any, blocks_ref, sems.at[4])] + [
        pltpu.make_async_copy(
            inverse_any.at[pl.ds(part * k, part)], inverse_ref.at[pl.ds(part * k, part)],
            sems.at[8 + k],
        )
        for k in range(8)
    ]
    for copy in first + later:
        copy.start()
    first[0].wait()
    place, order = raster(neighbor_ref[...])
    turned = pltpu.roll(order, HALF, 1)
    low = lax.broadcasted_iota(jnp.int32, (8, LANES), 1) < HALF
    lowest, highest = jnp.where(low, order, turned), jnp.where(low, turned, order)
    mine = jnp.where(core == 0, lowest, highest)
    other = jnp.where(core == 0, highest, lowest)
    mine_ref[...] = mine
    place_ref[...] = place
    mine, other = mine[0:1, :], other[0:1, :]
    for copy in first[1:]:
        copy.wait()
    fields = [forcing_ref[m] for m in range(STEPS)] + [gain_ref[0]]
    for m in range(0, STEPS, 2):
        out_ref[m // 2] = jnp.where(
            low_half(), columns(fields[m], other), columns(fields[m + 1], other)
        )
    out_ref[STEPS // 2] = columns(fields[STEPS], other)
    for m, field in enumerate(fields):
        own_ref[m] = columns(field, mine)
    start_ref[...] = columns(state_ref[...], mine)
    for copy in later:
        copy.wait()


def tables_kernel(mine_ref, blocks_ref, inverse_ref, faces_ref, table_ref, _):
    core = lax.axis_index("c")
    mine = jnp.concatenate([mine_ref[...]] * (VALUES // 8), axis=0)
    blocks = [blocks_ref[f] for f in range(4)]
    blocks += [
        jnp.where(core == 0, blocks_ref[4], blocks_ref[5]),
        jnp.where(core == 0, blocks_ref[5], blocks_ref[4]),
    ]
    for f, block in enumerate(blocks):
        high, low = halves(block)
        faces_ref[:VALUES, f * VALUES : (f + 1) * VALUES] = high
        faces_ref[VALUES:, f * VALUES : (f + 1) * VALUES] = low
    for j in range(VALUES):
        table_ref[j] = columns(inverse_ref[:, j, :], mine)


def packed(x):
    rows = VALUES // 2
    return jnp.where(low_half()[:rows], x[:rows], swap_halves(x)[rows:])


def unpacked(x):
    low, turned = low_half()[: VALUES // 2], swap_halves(x)
    return jnp.concatenate([jnp.where(low, x, turned), jnp.where(low, turned, x)], axis=0)


def first_kernel(
    lead, own_ref, got_ref, start_ref, table_ref, sources_ref, gain_ref, field_ref, right_ref, scratch
):
    core = lax.axis_index("c")
    low = low_half()
    is_own = low == (core == 0)
    for m in range(STEPS + 1):
        got = got_ref[m // 2]
        turned = swap_halves(got)
        if m % 2 == 0:
            other = jnp.where(core == 0, turned, got)
        else:
            other = jnp.where(core == 0, got, turned)
        value = jnp.where(is_own, own_ref[m], other)
        if m < STEPS:
            sources_ref[m] = value
        else:
            gain_ref[...] = value
    first = jnp.logical_and(low, lax.axis_index("q") == 0)
    right = jnp.where(first, start_ref[...], 0.0) + sources_ref[0]
    right_ref[...] = right
    begin(lead, right, table_ref, field_ref, scratch)


def begin(lead, right, table_ref, field_ref, scratch):
    @pl.when(lax.axis_index("c") == lead)
    def _field():
        field_ref[...] = apply_inverse(table_ref, scratch, right)

    @pl.when(lax.axis_index("c") != lead)
    def _later():
        field_ref[...] = jnp.zeros(FIELD, F32)


def late_kernel(lead, field_ref, right_ref, faces_ref, table_ref, field_out,
                ahead_ref, scratch):
    core = lax.axis_index("c")

    @pl.when(core != lead)
    def _run():
        field = apply_inverse(table_ref, scratch, right_ref[...])
        field_out[...] = field
        ahead_ref[...] = own_faces(field, faces_ref[...])

    @pl.when(core == lead)
    def _keep():
        field_out[...] = field_ref[...]


def ahead_kernel(active, pair_ref, faces_ref, ahead_ref, _):
    @pl.when(lax.axis_index("c") == active)
    def _run():
        ahead_ref[...] = own_faces(pair_ref[1], faces_ref[...])


def across_faces(faces, far, near):
    return product(faces[:, 4 * VALUES :], jnp.concatenate([far, near], axis=0))


def open_kernel(lead, field_ref, right_ref, ahead_ref, near_ref, far_ref, faces_ref, table_ref,
                pair_out, scratch):
    core = lax.axis_index("c")

    @pl.when(core != lead)
    def _run():
        summed = ahead_ref[...] + across_faces(faces_ref[...], far_ref[...], near_ref[...])
        pair_out[0] = field_ref[...]
        pair_out[1] = apply_inverse(table_ref, scratch, right_ref[...] - summed)

    @pl.when(core == lead)
    def _keep():
        pair_out[0] = jnp.zeros(FIELD, F32)
        pair_out[1] = field_ref[...]


def advance_kernel(stage, active, sourced, pair_ref, right_ref, ahead_ref, near_ref, far_ref,
                   faces_ref, table_ref, sources_ref, pair_out, right_out,
                   scratch):
    core = lax.axis_index("c")

    @pl.when(core == active)
    def _run():
        faces = faces_ref[...]
        far, near = (jnp.concatenate([ref[0], ref[1]], axis=1) for ref in (far_ref, near_ref))
        across = across_faces(faces, far, near)
        right = right_ref[...]

        def taken(summed, right, stage):
            field = apply_inverse(table_ref, scratch, right - summed)
            if stage % 2 == 1:
                right = field
                if sourced:
                    right = right + sources_ref[(stage + 1) // 2]
                field = apply_inverse(table_ref, scratch, right)
            return field, right

        field, right = taken(ahead_ref[...] + across[:, :LANES], right, stage)
        pair_out[0] = field
        summed = own_faces(field, faces) + across[:, LANES:]
        field, right = taken(summed, right, stage + 1)
        pair_out[1] = field
        right_out[...] = right

    @pl.when(core != active)
    def _keep():
        pair_out[...] = pair_ref[...]
        right_out[...] = right_ref[...]


def last_kernel(lead, pair_ref, right_ref, ahead_ref, near_ref, far_ref, faces_ref, table_ref,
                field_out, scratch):
    core = lax.axis_index("c")

    @pl.when(core == lead)
    def _run():
        summed = ahead_ref[...] + across_faces(faces_ref[...], far_ref[0], near_ref[0])
        field_out[...] = apply_inverse(table_ref, scratch, right_ref[...] - summed)

    @pl.when(core != lead)
    def _keep():
        field_out[...] = pair_ref[1]


def tail_kernel(lead, field_ref, right_ref, near_ref, far_ref, faces_ref,
                table_ref, out_ref, scratch):
    core = lax.axis_index("c")
    out_ref[...] = own_faces(field_ref[...], faces_ref[...])

    @pl.when(core == lead)
    def _run():
        summed = out_ref[...] + across_faces(faces_ref[...], far_ref[1], near_ref[1])
        out_ref[...] = apply_inverse(table_ref, scratch, right_ref[...] - summed)


def ends_kernel(lead, sourced, count, *refs):
    if sourced:
        (right_ref, tail_ref, near_ref, far_ref, faces_ref, table_ref, gain_ref, residual_ref,
         chunk_ref, scratch, end_ref) = refs
    else:
        (right_ref, tail_ref, near_ref, far_ref, faces_ref, table_ref, gain_ref, shift_ref,
         residual_ref, chunk_ref, scratch, end_ref) = refs
    core = lax.axis_index("c")

    @pl.when(core != lead)
    def _run():
        summed = tail_ref[...] + across_faces(faces_ref[...], far_ref[...], near_ref[...])
        end_ref[...] = apply_inverse(table_ref, scratch, right_ref[...] - summed)

    @pl.when(core == lead)
    def _keep():
        end_ref[...] = tail_ref[...]

    gain = gain_ref[...]
    residual = end_ref[...]
    if not sourced:
        residual = residual - gain * shift_ref[...]
    residual_ref[...] = residual
    rows = VALUES // 2
    chunk = packed(swap_halves(gain * swap_halves(residual) + residual))
    if sourced:
        gains = packed(gain * swap_halves(gain))
    for q in range(count):
        chunk_ref[q, :rows] = chunk
        if sourced:
            chunk_ref[q, rows:] = gains


def scanned(count, sums_ref, gains_ref):
    mine = lax.axis_index("q")
    rows = VALUES // 2
    before = jnp.zeros((rows, LANES), F32)
    for q in range(count):
        after = gains_ref[q, rows:] * before + sums_ref[q, :rows]
        before = jnp.where(q < mine, after, before)
    return unpacked(before)


def shifted(before, gain, residual):
    return jnp.where(low_half(), before, swap_halves(gain * before + residual))


def restart_kernel(
    lead, count, sums_ref, end_ref, gain_ref, table_ref, shift_ref, coarse_ref, field_ref, scratch
):
    gain, end = gain_ref[...], end_ref[...]
    shift = shifted(scanned(count, sums_ref, sums_ref), gain, end)
    shift_ref[...] = shift
    coarse_ref[...] = gain * shift + end
    begin(lead, shift, table_ref, field_ref, scratch)


def finish_kernel(count, sums_ref, gains_ref, residual_ref, gain_ref, coarse_ref, end_ref, out_ref, _):
    core = lax.axis_index("c")
    low = low_half()
    gain, residual = gain_ref[...], residual_ref[...]
    shift = shifted(scanned(count, sums_ref, gains_ref), gain, residual)
    end = coarse_ref[...] + (gain * shift + residual)
    end_ref[...] = end
    out_ref[...] = jnp.where(
        core == 0,
        jnp.where(low, swap_halves(end), residual),
        jnp.where(low, end, swap_halves(residual)),
    )


def output_kernel(end_ref, residual_ref, got_ref, place_ref, end_out, residual_out, _):
    core = lax.axis_index("c")
    low = low_half()
    got = got_ref[...]
    turned = swap_halves(got)
    end, residual = end_ref[...], residual_ref[...]
    end = jnp.where(core == 0, jnp.where(low, end, turned), jnp.where(low, got, end))
    residual = jnp.where(
        core == 0, jnp.where(low, residual, got), jnp.where(low, turned, residual)
    )
    place = place_ref[0:1, :]
    end_out[0] = columns(end, place)
    residual_out[0] = columns(residual, place)


def body(count, depth, initial_state, forcing, coarse_gain, block_inverse, face_blocks, neighbor, send_rows):
    def swap_cores(x):
        return lax.ppermute(x, "c", [(0, 1), (1, 0)])

    def halo(x, to):
        if to == 1:
            across = [(z + 1, depth + z) for z in range(depth - 1)]
        else:
            across = [(depth + z, z + 1) for z in range(depth - 1)]
        far = lax.ppermute(x, ("c", "space"), across)
        near = lax.ppermute(x, "c", [(1 - to, to)])
        return vmem(near), vmem(far)

    field, pair_shape = (FIELD, F32), ((2,) + FIELD, F32)
    index, raw = ((8, LANES), jnp.int32), (face_blocks, block_inverse)
    own, sent, start, mine, place, *raw = call(
        share_kernel, "share",
        [((STEPS + 1,) + FIELD, F32), ((STEPS // 2 + 1,) + FIELD, F32), field, index, index,
         *((x.shape, x.dtype) for x in raw)],
        *map(hbm, (neighbor, forcing, coarse_gain, initial_state, *raw)), fetch=True,
        scratch=(FIELD, forcing.shape, coarse_gain.shape), ints=(neighbor.shape,),
    )
    got = swap_cores(sent)
    faces, table = call(
        tables_kernel, "tables",
        [((2 * VALUES, 6 * VALUES), BF16), ((VALUES,) + FIELD, F32)], *map(vmem, (mine, *raw)),
    )
    operator = faces, table = vmem(faces), vmem(table)
    sources, gain, begun, right = call(
        functools.partial(first_kernel, 0), "first", [((STEPS,) + FIELD, F32), field, field, field],
        vmem(own), vmem(got), vmem(start), table,
    )
    sources, gain = vmem(sources), vmem(gain)

    def evolve(lead, now, right, sourced, shift):
        other = 1 - lead
        right = vmem(right)
        now = vmem(now)
        near, far = halo(now, other)
        now, ahead = call(
            functools.partial(late_kernel, lead), "late", [field, field], now, right, *operator
        )
        (pair,) = call(
            functools.partial(open_kernel, lead), "open", [pair_shape],
            vmem(now), right, vmem(ahead), near, far, faces, table,
        )
        for stage in range(STAGES - 1):
            active = (lead, other)[stage % 2]
            pair = vmem(pair)
            near, far = halo(pair, active)
            (ahead,) = call(
                functools.partial(ahead_kernel, active), "ahead", [field], pair, faces
            )
            ahead = vmem(ahead)
            if stage < STAGES - 2:
                pair, right = call(
                    functools.partial(advance_kernel, stage, active, sourced), "advance",
                    [pair_shape, field], pair, right, ahead, near, far, *operator, sources,
                )
                right = vmem(right)
        (now,) = call(
            functools.partial(last_kernel, lead), "last", [field],
            pair, right, ahead, near, far, faces, table,
        )
        now = vmem(now)
        tail_halo = near, far
        near, far = halo(now, other)
        (tail,) = call(
            functools.partial(tail_kernel, lead), "tail", [field], now, right, *tail_halo, *operator
        )
        rows = VALUES if sourced else VALUES // 2
        residual, chunk = call(
            functools.partial(ends_kernel, lead, sourced, count), "ends",
            [field, ((count, rows, LANES), F32)],
            right, vmem(tail), near, far, faces, table, gain, *shift, scratch=(FIELD, FIELD),
        )
        return vmem(residual), vmem(lax.all_to_all(chunk, "q", 0, 0))

    end, gains = evolve(0, begun, right, True, ())
    shift, coarse, begun = call(
        functools.partial(restart_kernel, 0, count), "restart", [field, field, field],
        gains, end, gain, table,
    )
    shift = vmem(shift)
    residual, sums = evolve(0, begun, shift, False, (shift,))
    end, sent = call(
        functools.partial(finish_kernel, count), "finish", [field, field],
        sums, gains, residual, gain, vmem(coarse),
    )
    got = vmem(swap_cores(sent))
    return call(
        output_kernel, "output", [((1,) + FIELD, F32)] * 2, vmem(end), residual, got, vmem(place),
        keep=False,
    )


def solution(mesh):
    slices, depth = mesh.devices.shape
    count = slices // 2
    pairs = Mesh(mesh.devices.reshape(count, 2, depth), ("q", "c", "space"))
    tm = ("q", "c")
    return jax.shard_map(
        functools.partial(body, count, depth),
        mesh=pairs,
        in_specs=(
            P(None, "space"),
            P(tm, None, "space"),
            P(tm, None, "space"),
            P(None, None, "space"),
            P(),
            P(None, "space"),
            P(None, "space"),
        ),
        out_specs=(P(tm, None, "space"), P(tm, None, "space")),
        check_vma=False,
    )
```

```python
import functools

import jax
import jax.numpy as jnp
from jax import lax
from jax.experimental import pallas as pl
from jax.experimental.pallas import tpu as pltpu
from jax.sharding import Mesh, PartitionSpec as P


VALUES = 64
LANES = 128
HALF = 64
STEPS = 4
STAGES = 2 * STEPS
GX = 8
GY = 8
SQUARED = 16
F32 = jnp.float32
BF16 = jnp.bfloat16
FIELD = (VALUES, LANES)


def vmem(x):
    return pltpu.with_memory_space_constraint(x, pltpu.VMEM)


def hbm(x):
    return pltpu.with_memory_space_constraint(x, pltpu.HBM)


def call(kernel, name, outs, *args, keep=True, fetch=False, alias={}, scratch=(FIELD,), ints=(), flops=1 << 22):
    whole = pl.BlockSpec(memory_space=pltpu.VMEM)
    shapes = tuple(
        pltpu.VMEM(shape, dtype) if keep else jax.ShapeDtypeStruct(shape, dtype)
        for shape, dtype in outs
    )
    held = [pltpu.VMEM(shape, F32) for shape in scratch]
    held += [pltpu.VMEM(shape, jnp.int32) for shape in ints]
    if fetch:
        held += [pltpu.SemaphoreType.DMA((16,))]
    return pl.pallas_call(
        kernel,
        out_shape=shapes,
        in_specs=[pl.BlockSpec(memory_space=pl.ANY) if fetch else whole] * len(args),
        out_specs=(whole,) * len(shapes),
        scratch_shapes=held,
        input_output_aliases=alias,
        cost_estimate=pl.CostEstimate(flops=flops, bytes_accessed=1 << 20, transcendentals=0),
        compiler_params=pltpu.CompilerParams(vmem_limit_bytes=16 << 20),
        name=name,
    )(*args)


def low_half():
    return lax.broadcasted_iota(jnp.int32, FIELD, 1) < HALF


def swap_halves(x):
    return pltpu.roll(x, HALF, 1)


def columns(x, index):
    return jnp.take_along_axis(x, jnp.broadcast_to(index, x.shape), axis=1)


def raster(neighbor):
    ahead = jnp.concatenate([neighbor, jnp.zeros((2, LANES), jnp.int32)], axis=0)
    level = jnp.where(ahead[4:5, :] >= LANES, 0, HALF)
    steps = (ahead >= 0).astype(jnp.int32)
    span = 1
    while span < max(GX, GY):
        on = ahead >= 0
        spot = jnp.clip(ahead, 0, LANES - 1)
        steps = steps + jnp.where(on, jnp.take_along_axis(steps, spot, axis=1), 0)
        ahead = jnp.where(on, jnp.take_along_axis(ahead, spot, axis=1), -1)
        span *= 2
    place = level + GX * steps[2:3, :] + steps[0:1, :]
    down = jnp.transpose(jnp.broadcast_to(place.astype(F32), (LANES, LANES)))
    across = lax.broadcasted_iota(jnp.int32, (LANES, LANES), 1).astype(F32)
    at = lax.broadcasted_iota(jnp.int32, (LANES, LANES), 0).astype(F32)
    order = jnp.sum(jnp.where(down == across, at, 0.0), axis=0, keepdims=True).astype(jnp.int32)
    return jnp.broadcast_to(place, (8, LANES)), jnp.broadcast_to(order, (8, LANES))


def apply_inverse(inverse_ref, scratch, vector):
    scratch[...] = vector
    total = inverse_ref[0] * scratch[0:1, :]
    for j in range(1, VALUES):
        total = total + inverse_ref[j] * scratch[j : j + 1, :]
    return total


def halves(x):
    high = x.astype(BF16)
    return high, (x - high.astype(F32)).astype(BF16)


def product(faces, layers):
    width = layers.shape[1]
    parts = jnp.dot(faces, jnp.concatenate(halves(layers), axis=1), preferred_element_type=F32)
    upper, lower = parts[:VALUES], parts[VALUES:]
    return upper[:, :width] + ((upper[:, width:] + lower[:, :width]) + lower[:, width:])


def own_faces(field, faces):
    lane = lax.broadcasted_iota(jnp.int32, FIELD, 1)
    x = jnp.bitwise_and(lane, GX - 1)
    y = jnp.bitwise_and(lane, GX * GY - GX)
    picked = [
        jnp.where(inside, pltpu.roll(field, by % LANES, 1), 0.0)
        for inside, by in ((x > 0, 1), (x < GX - 1, -1), (y > 0, GX), (y < GX * GY - GX, -GX))
    ]
    return product(faces[:, : 4 * VALUES], jnp.concatenate(picked, axis=0))


def share_kernel(neighbor_any, forcing_any, gain_any, state_any, blocks_any, inverse_any,
                 own_ref, out_ref, start_ref, mine_ref, place_ref, blocks_ref, inverse_ref,
                 state_ref, forcing_ref, gain_ref, neighbor_ref, sems):
    core = lax.axis_index("c")
    part = VALUES // 8
    first = [
        pltpu.make_async_copy(neighbor_any, neighbor_ref, sems.at[0]),
        pltpu.make_async_copy(forcing_any, forcing_ref, sems.at[1]),
        pltpu.make_async_copy(gain_any, gain_ref, sems.at[2]),
        pltpu.make_async_copy(state_any, state_ref, sems.at[3]),
    ]
    later = [pltpu.make_async_copy(blocks_any, blocks_ref, sems.at[4])] + [
        pltpu.make_async_copy(
            inverse_any.at[pl.ds(part * k, part)], inverse_ref.at[pl.ds(part * k, part)],
            sems.at[8 + k],
        )
        for k in range(8)
    ]
    for copy in first + later:
        copy.start()
    first[0].wait()
    place, order = raster(neighbor_ref[...])
    turned = pltpu.roll(order, HALF, 1)
    low = lax.broadcasted_iota(jnp.int32, (8, LANES), 1) < HALF
    lowest, highest = jnp.where(low, order, turned), jnp.where(low, turned, order)
    mine = jnp.where(core == 0, lowest, highest)
    other = jnp.where(core == 0, highest, lowest)
    mine_ref[...] = mine
    place_ref[...] = place
    mine, other = mine[0:1, :], other[0:1, :]
    for copy in first[1:]:
        copy.wait()
    fields = [forcing_ref[m] for m in range(STEPS)] + [gain_ref[0]]
    for m in range(0, STEPS, 2):
        out_ref[m // 2] = jnp.where(
            low_half(), columns(fields[m], other), columns(fields[m + 1], other)
        )
    out_ref[STEPS // 2] = columns(fields[STEPS], other)
    for m, field in enumerate(fields):
        own_ref[m] = columns(field, mine)
    start_ref[...] = columns(state_ref[...], mine)
    for copy in later:
        copy.wait()


def tables_kernel(mine_ref, blocks_ref, inverse_ref, faces_ref, table_ref, _):
    core = lax.axis_index("c")
    mine = jnp.concatenate([mine_ref[...]] * (VALUES // 8), axis=0)
    blocks = [blocks_ref[f] for f in range(4)]
    blocks += [
        jnp.where(core == 0, blocks_ref[4], blocks_ref[5]),
        jnp.where(core == 0, blocks_ref[5], blocks_ref[4]),
    ]
    for f, block in enumerate(blocks):
        high, low = halves(block)
        faces_ref[:VALUES, f * VALUES : (f + 1) * VALUES] = high
        faces_ref[VALUES:, f * VALUES : (f + 1) * VALUES] = low
    for j in range(VALUES):
        table_ref[j] = columns(inverse_ref[:, j, :], mine)


def packed(x):
    rows = VALUES // 2
    return jnp.where(low_half()[:rows], x[:rows], swap_halves(x)[rows:])


def unpacked(x):
    low, turned = low_half()[: VALUES // 2], swap_halves(x)
    return jnp.concatenate([jnp.where(low, x, turned), jnp.where(low, turned, x)], axis=0)


def first_kernel(
    lead, own_ref, got_ref, start_ref, table_ref, sources_ref, gain_ref, field_ref, right_ref, scratch
):
    core = lax.axis_index("c")
    low = low_half()
    is_own = low == (core == 0)
    for m in range(STEPS + 1):
        got = got_ref[m // 2]
        turned = swap_halves(got)
        if m % 2 == 0:
            other = jnp.where(core == 0, turned, got)
        else:
            other = jnp.where(core == 0, got, turned)
        value = jnp.where(is_own, own_ref[m], other)
        if m < STEPS:
            sources_ref[m] = value
        else:
            gain_ref[...] = value
    first = jnp.logical_and(low, lax.axis_index("q") == 0)
    right = jnp.where(first, start_ref[...], 0.0) + sources_ref[0]
    right_ref[...] = right
    begin(lead, right, table_ref, field_ref, scratch)


def begin(lead, right, table_ref, field_ref, scratch):
    @pl.when(lax.axis_index("c") == lead)
    def _field():
        field_ref[...] = apply_inverse(table_ref, scratch, right)

    @pl.when(lax.axis_index("c") != lead)
    def _later():
        field_ref[...] = jnp.zeros(FIELD, F32)


def late_kernel(lead, field_ref, right_ref, faces_ref, table_ref, field_out,
                ahead_ref, scratch):
    core = lax.axis_index("c")

    @pl.when(core != lead)
    def _run():
        field = apply_inverse(table_ref, scratch, right_ref[...])
        field_out[...] = field
        ahead_ref[...] = own_faces(field, faces_ref[...])

    @pl.when(core == lead)
    def _keep():
        field_out[...] = field_ref[...]


def ahead_right_kernel(active, left, pair_ref, right_ref, faces_ref, table_ref, ahead_ref, right_out, scratch):
    @pl.when(lax.axis_index("c") == active)
    def _run():
        ahead_ref[...] = own_faces(pair_ref[1], faces_ref[...])
        right_out[...] = right_ref[...]

    @pl.when(lax.axis_index("c") != active)
    def _right():
        if left:
            right_out[...] = apply_inverse(table_ref, scratch, right_ref[...])
        else:
            right_out[...] = right_ref[...]


def square(begin, table_ref, square_ref, scratch):
    @pl.loop(begin, begin + SQUARED)
    def _column(j):
        square_ref[j] = apply_inverse(table_ref, scratch, table_ref[j])


def ahead_square_kernel(active, begin, pair_ref, faces_ref, table_ref, *refs):
    ahead_ref, square_ref, scratch = refs[-3:]

    @pl.when(lax.axis_index("c") == active)
    def _run():
        ahead_ref[...] = own_faces(pair_ref[1], faces_ref[...])
        square(begin, table_ref, square_ref, scratch)


def across_faces(faces, far, near):
    return product(faces[:, 4 * VALUES :], jnp.concatenate([far, near], axis=0))


def open_kernel(lead, field_ref, right_ref, ahead_ref, near_ref, far_ref, faces_ref, table_ref,
                pair_out, scratch):
    core = lax.axis_index("c")

    @pl.when(core != lead)
    def _run():
        summed = ahead_ref[...] + across_faces(faces_ref[...], far_ref[...], near_ref[...])
        pair_out[0] = field_ref[...]
        pair_out[1] = apply_inverse(table_ref, scratch, right_ref[...] - summed)

    @pl.when(core == lead)
    def _keep():
        pair_out[0] = jnp.zeros(FIELD, F32)
        pair_out[1] = field_ref[...]


def advance_kernel(stage, active, sourced, pair_ref, right_ref, ahead_ref, near_ref, far_ref,
                   faces_ref, table_ref, sources_ref, pair_out, right_out,
                   scratch):
    core = lax.axis_index("c")

    @pl.when(core == active)
    def _run():
        faces = faces_ref[...]
        far, near = (jnp.concatenate([ref[0], ref[1]], axis=1) for ref in (far_ref, near_ref))
        across = across_faces(faces, far, near)
        right = right_ref[...]

        def taken(summed, right, stage):
            field = apply_inverse(table_ref, scratch, right - summed)
            if stage % 2 == 1:
                right = field
                if sourced:
                    right = right + sources_ref[(stage + 1) // 2]
                field = apply_inverse(table_ref, scratch, right)
            return field, right

        field, right = taken(ahead_ref[...] + across[:, :LANES], right, stage)
        pair_out[0] = field
        summed = own_faces(field, faces) + across[:, LANES:]
        field, right = taken(summed, right, stage + 1)
        pair_out[1] = field
        right_out[...] = right

    @pl.when(core != active)
    def _keep():
        pair_out[...] = pair_ref[...]
        right_out[...] = right_ref[...]


def advance_squared_kernel(stage, active, pair_ref, right_ref, ahead_ref, near_ref, far_ref,
                           faces_ref, table_ref, square_ref, pair_out, right_out, scratch, other):
    core = lax.axis_index("c")

    @pl.when(core == active)
    def _run():
        faces = faces_ref[...]
        far, near = (jnp.concatenate([ref[0], ref[1]], axis=1) for ref in (far_ref, near_ref))
        across = across_faces(faces, far, near)
        right = right_ref[...]
        vector = right - (ahead_ref[...] + across[:, :LANES])
        if stage % 2 == 0:
            field = apply_inverse(table_ref, scratch, vector)
            pair_out[0] = field
            vector = right - (own_faces(field, faces) + across[:, LANES:])
            pair_out[1] = apply_inverse(square_ref, other, vector)
            right_out[...] = vector
        else:
            field = apply_inverse(square_ref, scratch, vector)
            pair_out[0] = field
            right = apply_inverse(table_ref, scratch, vector)
            right_out[...] = right
            vector = right - (own_faces(field, faces) + across[:, LANES:])
            pair_out[1] = apply_inverse(table_ref, other, vector)

    @pl.when(core != active)
    def _keep():
        pair_out[...] = pair_ref[...]
        right_out[...] = right_ref[...]


def last_kernel(lead, pair_ref, right_ref, ahead_ref, near_ref, far_ref, faces_ref, table_ref,
                field_out, scratch):
    core = lax.axis_index("c")

    @pl.when(core == lead)
    def _run():
        summed = ahead_ref[...] + across_faces(faces_ref[...], far_ref[0], near_ref[0])
        field_out[...] = apply_inverse(table_ref, scratch, right_ref[...] - summed)

    @pl.when(core != lead)
    def _keep():
        field_out[...] = pair_ref[1]


def tail_kernel(lead, begin, field_ref, right_ref, near_ref, far_ref, faces_ref, table_ref, *refs):
    if begin is None:
        out_ref, scratch = refs
    else:
        _, out_ref, square_ref, scratch = refs
    core = lax.axis_index("c")
    out_ref[...] = own_faces(field_ref[...], faces_ref[...])

    @pl.when(core == lead)
    def _run():
        summed = out_ref[...] + across_faces(faces_ref[...], far_ref[1], near_ref[1])
        out_ref[...] = apply_inverse(table_ref, scratch, right_ref[...] - summed)

    if begin is not None:
        @pl.when(core != lead)
        def _square():
            square(begin, table_ref, square_ref, scratch)


def ends_kernel(lead, sourced, count, *refs):
    if sourced:
        (right_ref, tail_ref, near_ref, far_ref, faces_ref, table_ref, gain_ref, residual_ref,
         chunk_ref, scratch, end_ref) = refs
    else:
        (right_ref, tail_ref, near_ref, far_ref, faces_ref, table_ref, gain_ref, shift_ref,
         residual_ref, chunk_ref, scratch, end_ref) = refs
    core = lax.axis_index("c")

    @pl.when(core != lead)
    def _run():
        summed = tail_ref[...] + across_faces(faces_ref[...], far_ref[...], near_ref[...])
        end_ref[...] = apply_inverse(table_ref, scratch, right_ref[...] - summed)

    @pl.when(core == lead)
    def _keep():
        end_ref[...] = tail_ref[...]

    gain = gain_ref[...]
    residual = end_ref[...]
    if not sourced:
        residual = residual - gain * shift_ref[...]
    residual_ref[...] = residual
    rows = VALUES // 2
    chunk = packed(swap_halves(gain * swap_halves(residual) + residual))
    if sourced:
        gains = packed(gain * swap_halves(gain))
    for q in range(count):
        chunk_ref[q, :rows] = chunk
        if sourced:
            chunk_ref[q, rows:] = gains


def scanned(count, sums_ref, gains_ref):
    mine = lax.axis_index("q")
    rows = VALUES // 2
    before = jnp.zeros((rows, LANES), F32)
    for q in range(count):
        after = gains_ref[q, rows:] * before + sums_ref[q, :rows]
        before = jnp.where(q < mine, after, before)
    return unpacked(before)


def shifted(before, gain, residual):
    return jnp.where(low_half(), before, swap_halves(gain * before + residual))


def restart_kernel(lead, sums_ref, end_ref, gain_ref, table_ref, field_ref, scratch):
    @pl.when(lax.axis_index("c") == lead)
    def _field():
        before = scanned(sums_ref.shape[0], sums_ref, sums_ref)
        shift = shifted(before, gain_ref[...], end_ref[...])
        field_ref[...] = apply_inverse(table_ref, scratch, shift)

    @pl.when(lax.axis_index("c") != lead)
    def _later():
        field_ref[...] = jnp.zeros(FIELD, F32)


def late_restart_kernel(lead, field_ref, sums_ref, end_ref, gain_ref, faces_ref, table_ref, field_out,
                        ahead_ref, shift_ref, coarse_ref, scratch):
    gain, end = gain_ref[...], end_ref[...]
    shift = shifted(scanned(sums_ref.shape[0], sums_ref, sums_ref), gain, end)
    shift_ref[...] = shift
    coarse_ref[...] = gain * shift + end
    late_kernel(lead, field_ref, shift_ref, faces_ref, table_ref, field_out, ahead_ref, scratch)


def finish_kernel(count, sums_ref, gains_ref, residual_ref, gain_ref, coarse_ref, end_ref, out_ref, _):
    core = lax.axis_index("c")
    low = low_half()
    gain, residual = gain_ref[...], residual_ref[...]
    shift = shifted(scanned(count, sums_ref, gains_ref), gain, residual)
    end = coarse_ref[...] + (gain * shift + residual)
    end_ref[...] = end
    out_ref[...] = jnp.where(
        core == 0,
        jnp.where(low, swap_halves(end), residual),
        jnp.where(low, end, swap_halves(residual)),
    )


def output_kernel(end_ref, residual_ref, got_ref, place_ref, end_out, residual_out, _):
    core = lax.axis_index("c")
    low = low_half()
    got = got_ref[...]
    turned = swap_halves(got)
    end, residual = end_ref[...], residual_ref[...]
    end = jnp.where(core == 0, jnp.where(low, end, turned), jnp.where(low, got, end))
    residual = jnp.where(
        core == 0, jnp.where(low, residual, got), jnp.where(low, turned, residual)
    )
    place = place_ref[0:1, :]
    end_out[0] = columns(end, place)
    residual_out[0] = columns(residual, place)


def body(count, depth, initial_state, forcing, coarse_gain, block_inverse, face_blocks, neighbor, send_rows):
    def swap_cores(x):
        return lax.ppermute(x, "c", [(0, 1), (1, 0)])

    def halo(x, to):
        if to == 1:
            across = [(z + 1, depth + z) for z in range(depth - 1)]
        else:
            across = [(depth + z, z + 1) for z in range(depth - 1)]
        far = lax.ppermute(x, ("c", "space"), across)
        near = lax.ppermute(x, "c", [(1 - to, to)])
        return vmem(near), vmem(far)

    lead, other = 0, 1
    field, pair_shape = (FIELD, F32), ((2,) + FIELD, F32)
    index, raw = ((8, LANES), jnp.int32), (face_blocks, block_inverse)
    own, sent, start, mine, place, *raw = call(
        share_kernel, "share",
        [((STEPS + 1,) + FIELD, F32), ((STEPS // 2 + 1,) + FIELD, F32), field, index, index,
         *((x.shape, x.dtype) for x in raw)],
        *map(hbm, (neighbor, forcing, coarse_gain, initial_state, *raw)), fetch=True,
        scratch=(FIELD, forcing.shape, coarse_gain.shape), ints=(neighbor.shape,),
    )
    got = swap_cores(sent)
    faces, table = call(
        tables_kernel, "tables",
        [((2 * VALUES, 6 * VALUES), BF16), ((VALUES,) + FIELD, F32)], *map(vmem, (mine, *raw)),
    )
    operator = faces, table = vmem(faces), vmem(table)
    sources, gain, begun, right = call(
        functools.partial(first_kernel, lead), "first", [((STEPS,) + FIELD, F32), field, field, field],
        vmem(own), vmem(got), vmem(start), table,
    )
    sources, gain = vmem(sources), vmem(gain)

    def evolve(now, right=None, restart=(), squared=None):
        sourced = squared is None
        now = vmem(now)
        near, far = halo(now, other)
        if sourced:
            right = vmem(right)
            now, ahead = call(
                functools.partial(late_kernel, lead), "late", [field] * 2, now, right, *operator
            )
        else:
            now, ahead, right, coarse = call(
                functools.partial(late_restart_kernel, lead), "late", [field] * 4, now, *restart,
                *operator,
            )
            right = shift = vmem(right)
        (pair,) = call(
            functools.partial(open_kernel, lead), "open", [pair_shape],
            vmem(now), right, vmem(ahead), near, far, *operator,
        )
        for stage in range(STAGES - 1):
            active = (lead, other)[stage % 2]
            pair = vmem(pair)
            near, far = halo(pair, active)
            if sourced:
                ahead, squared = call(
                    functools.partial(ahead_square_kernel, active, stage // 2 * SQUARED), "ahead",
                    [field, square_shape], pair, *operator, *(() if stage == 0 else (squared,)),
                    alias={} if stage == 0 else {3: 1},
                )
                squared = vmem(squared)
            else:
                left = active == other and stage < STAGES - 2
                ahead, right = call(
                    functools.partial(ahead_right_kernel, active, left), "ahead", [field] * 2,
                    pair, right, *operator,
                )
                right = vmem(right)
            ahead = vmem(ahead)
            args = pair, right, ahead, near, far, *operator
            if stage < STAGES - 2:
                if sourced:
                    pair, right = call(
                        functools.partial(advance_kernel, stage, active, True), "advance",
                        [pair_shape, field], *args, sources,
                    )
                else:
                    pair, right = call(
                        functools.partial(advance_squared_kernel, stage, active), "advance",
                        [pair_shape, field], *args, squared, scratch=(FIELD, FIELD),
                    )
                right = vmem(right)
        (now,) = call(functools.partial(last_kernel, lead), "last", [field], *args)
        now = vmem(now)
        args = now, right, near, far, *operator
        near, far = halo(now, other)
        if sourced:
            tail, squared = call(
                functools.partial(tail_kernel, lead, VALUES - SQUARED), "tail",
                [field, square_shape], *args, squared, alias={6: 1},
            )
        else:
            (tail,) = call(functools.partial(tail_kernel, lead, None), "tail", [field], *args)
        rows = VALUES if sourced else VALUES // 2
        residual, chunk = call(
            functools.partial(ends_kernel, lead, sourced, count), "ends",
            [field, ((count, rows, LANES), F32)],
            right, vmem(tail), near, far, *operator, gain, *(() if sourced else (shift,)),
            scratch=(FIELD, FIELD),
        )
        gathered = vmem(lax.all_to_all(chunk, "q", 0, 0))
        return vmem(residual), gathered, vmem(squared) if sourced else coarse

    square_shape = ((VALUES,) + FIELD, F32)
    end, gains, squared = evolve(begun, right)
    restart = gains, end, gain
    (begun,) = call(
        functools.partial(restart_kernel, lead), "restart", [field], *restart, table
    )
    residual, sums, coarse = evolve(begun, restart=restart, squared=squared)
    end, sent = call(
        functools.partial(finish_kernel, count), "finish", [field, field],
        sums, gains, residual, gain, vmem(coarse),
    )
    got = vmem(swap_cores(sent))
    return call(
        output_kernel, "output", [((1,) + FIELD, F32)] * 2, vmem(end), residual, got, vmem(place),
        keep=False,
    )


def solution(mesh):
    slices, depth = mesh.devices.shape
    count = slices // 2
    pairs = Mesh(mesh.devices.reshape(count, 2, depth), ("q", "c", "space"))
    tm = ("q", "c")
    return jax.shard_map(
        functools.partial(body, count, depth),
        mesh=pairs,
        in_specs=(
            P(None, "space"),
            P(tm, None, "space"),
            P(tm, None, "space"),
            P(None, None, "space"),
            P(),
            P(None, "space"),
            P(None, "space"),
        ),
        out_specs=(P(tm, None, "space"), P(tm, None, "space")),
        check_vma=False,
    )
```

```python
import functools

import jax
import jax.numpy as jnp
from jax import lax
from jax.experimental import pallas as pl
from jax.experimental.pallas import tpu as pltpu
from jax.sharding import Mesh, PartitionSpec as P


VALUES = 64
LANES = 128
HALF = 64
STEPS = 4
STAGES = 2 * STEPS
GX = 8
GY = 8
SQUARED = 16
EARLY = 16
F32 = jnp.float32
BF16 = jnp.bfloat16
FIELD = (VALUES, LANES)


def vmem(x):
    return pltpu.with_memory_space_constraint(x, pltpu.VMEM)


def hbm(x):
    return pltpu.with_memory_space_constraint(x, pltpu.HBM)


def call(kernel, name, outs, *args, keep=True, fetch=False, alias={}, scratch=(FIELD,), ints=(), flops=1 << 22):
    whole = pl.BlockSpec(memory_space=pltpu.VMEM)
    shapes = tuple(
        pltpu.VMEM(shape, dtype) if keep else jax.ShapeDtypeStruct(shape, dtype)
        for shape, dtype in outs
    )
    held = [pltpu.VMEM(shape, F32) for shape in scratch]
    held += [pltpu.VMEM(shape, jnp.int32) for shape in ints]
    if fetch:
        held += [pltpu.SemaphoreType.DMA((16,))]
    return pl.pallas_call(
        kernel,
        out_shape=shapes,
        in_specs=[pl.BlockSpec(memory_space=pl.ANY) if fetch else whole] * len(args),
        out_specs=(whole,) * len(shapes),
        scratch_shapes=held,
        input_output_aliases=alias,
        cost_estimate=pl.CostEstimate(flops=flops, bytes_accessed=1 << 20, transcendentals=0),
        compiler_params=pltpu.CompilerParams(vmem_limit_bytes=16 << 20),
        name=name,
    )(*args)


def low_half():
    return lax.broadcasted_iota(jnp.int32, FIELD, 1) < HALF


def swap_halves(x):
    return pltpu.roll(x, HALF, 1)


def columns(x, index):
    return jnp.take_along_axis(x, jnp.broadcast_to(index, x.shape), axis=1)


def raster(neighbor):
    ahead = jnp.concatenate([neighbor, jnp.zeros((2, LANES), jnp.int32)], axis=0)
    level = jnp.where(ahead[4:5, :] >= LANES, 0, HALF)
    steps = (ahead >= 0).astype(jnp.int32)
    span = 1
    while span < max(GX, GY):
        on = ahead >= 0
        spot = jnp.clip(ahead, 0, LANES - 1)
        steps = steps + jnp.where(on, jnp.take_along_axis(steps, spot, axis=1), 0)
        ahead = jnp.where(on, jnp.take_along_axis(ahead, spot, axis=1), -1)
        span *= 2
    place = level + GX * steps[2:3, :] + steps[0:1, :]
    down = jnp.transpose(jnp.broadcast_to(place.astype(F32), (LANES, LANES)))
    across = lax.broadcasted_iota(jnp.int32, (LANES, LANES), 1).astype(F32)
    at = lax.broadcasted_iota(jnp.int32, (LANES, LANES), 0).astype(F32)
    order = jnp.sum(jnp.where(down == across, at, 0.0), axis=0, keepdims=True).astype(jnp.int32)
    return jnp.broadcast_to(place, (8, LANES)), jnp.broadcast_to(order, (8, LANES))


def apply_inverse(inverse_ref, scratch, vector):
    scratch[...] = vector
    total = inverse_ref[0] * scratch[0:1, :]
    for j in range(1, VALUES):
        total = total + inverse_ref[j] * scratch[j : j + 1, :]
    return total


def halves(x):
    high = x.astype(BF16)
    return high, (x - high.astype(F32)).astype(BF16)


def product(faces, layers):
    width = layers.shape[1]
    parts = jnp.dot(faces, jnp.concatenate(halves(layers), axis=1), preferred_element_type=F32)
    upper, lower = parts[:VALUES], parts[VALUES:]
    return upper[:, :width] + ((upper[:, width:] + lower[:, :width]) + lower[:, width:])


def own_faces(field, faces):
    lane = lax.broadcasted_iota(jnp.int32, FIELD, 1)
    x = jnp.bitwise_and(lane, GX - 1)
    y = jnp.bitwise_and(lane, GX * GY - GX)
    picked = [
        jnp.where(inside, pltpu.roll(field, by % LANES, 1), 0.0)
        for inside, by in ((x > 0, 1), (x < GX - 1, -1), (y > 0, GX), (y < GX * GY - GX, -GX))
    ]
    return product(faces[:, : 4 * VALUES], jnp.concatenate(picked, axis=0))


def share_kernel(neighbor_any, forcing_any, gain_any, state_any, blocks_any, inverse_any,
                 own_ref, out_ref, start_ref, mine_ref, place_ref, blocks_ref, rest_ref, table_ref,
                 state_ref, forcing_ref, gain_ref, early_ref, neighbor_ref, sems):
    core = lax.axis_index("c")
    part = VALUES // 8
    first = [
        pltpu.make_async_copy(neighbor_any, neighbor_ref, sems.at[0]),
        pltpu.make_async_copy(forcing_any, forcing_ref, sems.at[1]),
        pltpu.make_async_copy(gain_any, gain_ref, sems.at[2]),
        pltpu.make_async_copy(state_any, state_ref, sems.at[3]),
    ]
    early, later = (
        [
            pltpu.make_async_copy(
                inverse_any.at[pl.ds(begin + part * k, part)], ref.at[pl.ds(part * k, part)],
                sems.at[8 + begin // part + k],
            )
            for k in range(count)
        ]
        for begin, ref, count in (
            (0, early_ref, EARLY // part), (EARLY, rest_ref, (VALUES - EARLY) // part)
        )
    )
    later.append(pltpu.make_async_copy(blocks_any, blocks_ref, sems.at[4]))
    for copy in first + early + later:
        copy.start()
    first[0].wait()
    place, order = raster(neighbor_ref[...])
    turned = pltpu.roll(order, HALF, 1)
    low = lax.broadcasted_iota(jnp.int32, (8, LANES), 1) < HALF
    lowest, highest = jnp.where(low, order, turned), jnp.where(low, turned, order)
    mine = jnp.where(core == 0, lowest, highest)
    other = jnp.where(core == 0, highest, lowest)
    mine_ref[...] = mine
    place_ref[...] = place
    mine, other = mine[0:1, :], other[0:1, :]
    for copy in first[1:]:
        copy.wait()
    fields = [forcing_ref[m] for m in range(STEPS)] + [gain_ref[0]]
    for m in range(0, STEPS, 2):
        out_ref[m // 2] = jnp.where(
            low_half(), columns(fields[m], other), columns(fields[m + 1], other)
        )
    out_ref[STEPS // 2] = columns(fields[STEPS], other)
    for m, field in enumerate(fields):
        own_ref[m] = columns(field, mine)
    start_ref[...] = columns(state_ref[...], mine)
    for k, copy in enumerate(early):
        copy.wait()
        rows = pl.ds(part * k, part)
        for j in range(VALUES):
            table_ref[j, rows] = columns(early_ref[rows, j, :], mine)
    for copy in later:
        copy.wait()


def tables_kernel(mine_ref, blocks_ref, rest_ref, _table, faces_ref, table_ref, _):
    core = lax.axis_index("c")
    mine = jnp.concatenate([mine_ref[...]] * ((VALUES - EARLY) // 8), axis=0)
    blocks = [blocks_ref[f] for f in range(4)]
    blocks += [
        jnp.where(core == 0, blocks_ref[4], blocks_ref[5]),
        jnp.where(core == 0, blocks_ref[5], blocks_ref[4]),
    ]
    for f, block in enumerate(blocks):
        high, low = halves(block)
        faces_ref[:VALUES, f * VALUES : (f + 1) * VALUES] = high
        faces_ref[VALUES:, f * VALUES : (f + 1) * VALUES] = low
    for j in range(VALUES):
        table_ref[j, EARLY:] = columns(rest_ref[:, j, :], mine)


def packed(x):
    rows = VALUES // 2
    return jnp.where(low_half()[:rows], x[:rows], swap_halves(x)[rows:])


def unpacked(x):
    low, turned = low_half()[: VALUES // 2], swap_halves(x)
    return jnp.concatenate([jnp.where(low, x, turned), jnp.where(low, turned, x)], axis=0)


def first_kernel(
    lead, own_ref, got_ref, start_ref, table_ref, sources_ref, gain_ref, field_ref, right_ref, scratch
):
    core = lax.axis_index("c")
    low = low_half()
    is_own = low == (core == 0)
    for m in range(STEPS + 1):
        got = got_ref[m // 2]
        turned = swap_halves(got)
        if m % 2 == 0:
            other = jnp.where(core == 0, turned, got)
        else:
            other = jnp.where(core == 0, got, turned)
        value = jnp.where(is_own, own_ref[m], other)
        if m < STEPS:
            sources_ref[m] = value
        else:
            gain_ref[...] = value
    first = jnp.logical_and(low, lax.axis_index("q") == 0)
    right = jnp.where(first, start_ref[...], 0.0) + sources_ref[0]
    right_ref[...] = right
    begin(lead, right, table_ref, field_ref, scratch)


def begin(lead, right, table_ref, field_ref, scratch):
    @pl.when(lax.axis_index("c") == lead)
    def _field():
        field_ref[...] = apply_inverse(table_ref, scratch, right)

    @pl.when(lax.axis_index("c") != lead)
    def _later():
        field_ref[...] = jnp.zeros(FIELD, F32)


def late_kernel(lead, field_ref, right_ref, faces_ref, table_ref, field_out,
                ahead_ref, scratch):
    core = lax.axis_index("c")

    @pl.when(core != lead)
    def _run():
        field = apply_inverse(table_ref, scratch, right_ref[...])
        field_out[...] = field
        ahead_ref[...] = own_faces(field, faces_ref[...])

    @pl.when(core == lead)
    def _keep():
        field_out[...] = field_ref[...]


def ahead_right_kernel(active, left, pair_ref, right_ref, faces_ref, table_ref, ahead_ref, right_out, scratch):
    @pl.when(lax.axis_index("c") == active)
    def _run():
        ahead_ref[...] = own_faces(pair_ref[1], faces_ref[...])
        right_out[...] = right_ref[...]

    @pl.when(lax.axis_index("c") != active)
    def _right():
        if left:
            right_out[...] = apply_inverse(table_ref, scratch, right_ref[...])
        else:
            right_out[...] = right_ref[...]


def square(begin, table_ref, square_ref, scratch):
    @pl.loop(begin, begin + SQUARED)
    def _column(j):
        square_ref[j] = apply_inverse(table_ref, scratch, table_ref[j])


def ahead_square_kernel(active, begin, pair_ref, faces_ref, table_ref, *refs):
    ahead_ref, square_ref, scratch = refs[-3:]

    @pl.when(lax.axis_index("c") == active)
    def _run():
        ahead_ref[...] = own_faces(pair_ref[1], faces_ref[...])
        square(begin, table_ref, square_ref, scratch)


def across_faces(faces, far, near):
    return product(faces[:, 4 * VALUES :], jnp.concatenate([far, near], axis=0))


def open_kernel(lead, field_ref, right_ref, ahead_ref, near_ref, far_ref, faces_ref, table_ref,
                pair_out, scratch):
    core = lax.axis_index("c")

    @pl.when(core != lead)
    def _run():
        summed = ahead_ref[...] + across_faces(faces_ref[...], far_ref[...], near_ref[...])
        pair_out[0] = field_ref[...]
        pair_out[1] = apply_inverse(table_ref, scratch, right_ref[...] - summed)

    @pl.when(core == lead)
    def _keep():
        pair_out[0] = jnp.zeros(FIELD, F32)
        pair_out[1] = field_ref[...]


def advance_kernel(stage, active, sourced, pair_ref, right_ref, ahead_ref, near_ref, far_ref,
                   faces_ref, table_ref, sources_ref, pair_out, right_out,
                   scratch):
    core = lax.axis_index("c")

    @pl.when(core == active)
    def _run():
        faces = faces_ref[...]
        far, near = (jnp.concatenate([ref[0], ref[1]], axis=1) for ref in (far_ref, near_ref))
        across = across_faces(faces, far, near)
        right = right_ref[...]

        def taken(summed, right, stage):
            field = apply_inverse(table_ref, scratch, right - summed)
            if stage % 2 == 1:
                right = field
                if sourced:
                    right = right + sources_ref[(stage + 1) // 2]
                field = apply_inverse(table_ref, scratch, right)
            return field, right

        field, right = taken(ahead_ref[...] + across[:, :LANES], right, stage)
        pair_out[0] = field
        summed = own_faces(field, faces) + across[:, LANES:]
        field, right = taken(summed, right, stage + 1)
        pair_out[1] = field
        right_out[...] = right

    @pl.when(core != active)
    def _keep():
        pair_out[...] = pair_ref[...]
        right_out[...] = right_ref[...]


def advance_squared_kernel(stage, active, pair_ref, right_ref, ahead_ref, near_ref, far_ref,
                           faces_ref, table_ref, square_ref, pair_out, right_out, scratch, other):
    core = lax.axis_index("c")

    @pl.when(core == active)
    def _run():
        faces = faces_ref[...]
        far, near = (jnp.concatenate([ref[0], ref[1]], axis=1) for ref in (far_ref, near_ref))
        across = across_faces(faces, far, near)
        right = right_ref[...]
        vector = right - (ahead_ref[...] + across[:, :LANES])
        if stage % 2 == 0:
            field = apply_inverse(table_ref, scratch, vector)
            pair_out[0] = field
            vector = right - (own_faces(field, faces) + across[:, LANES:])
            pair_out[1] = apply_inverse(square_ref, other, vector)
            right_out[...] = vector
        else:
            field = apply_inverse(square_ref, scratch, vector)
            pair_out[0] = field
            right = apply_inverse(table_ref, scratch, vector)
            right_out[...] = right
            vector = right - (own_faces(field, faces) + across[:, LANES:])
            pair_out[1] = apply_inverse(table_ref, other, vector)

    @pl.when(core != active)
    def _keep():
        pair_out[...] = pair_ref[...]
        right_out[...] = right_ref[...]


def last_kernel(lead, pair_ref, right_ref, ahead_ref, near_ref, far_ref, faces_ref, table_ref,
                field_out, scratch):
    core = lax.axis_index("c")

    @pl.when(core == lead)
    def _run():
        summed = ahead_ref[...] + across_faces(faces_ref[...], far_ref[0], near_ref[0])
        field_out[...] = apply_inverse(table_ref, scratch, right_ref[...] - summed)

    @pl.when(core != lead)
    def _keep():
        field_out[...] = pair_ref[1]


def tail_kernel(lead, begin, field_ref, right_ref, near_ref, far_ref, faces_ref, table_ref, *refs):
    if begin is None:
        out_ref, scratch = refs
    else:
        _, out_ref, square_ref, scratch = refs
    core = lax.axis_index("c")
    out_ref[...] = own_faces(field_ref[...], faces_ref[...])

    @pl.when(core == lead)
    def _run():
        summed = out_ref[...] + across_faces(faces_ref[...], far_ref[1], near_ref[1])
        out_ref[...] = apply_inverse(table_ref, scratch, right_ref[...] - summed)

    if begin is not None:
        @pl.when(core != lead)
        def _square():
            square(begin, table_ref, square_ref, scratch)


def ends_kernel(lead, sourced, count, *refs):
    if sourced:
        (right_ref, tail_ref, near_ref, far_ref, faces_ref, table_ref, gain_ref, residual_ref,
         chunk_ref, scratch, end_ref) = refs
    else:
        (right_ref, tail_ref, near_ref, far_ref, faces_ref, table_ref, gain_ref, shift_ref,
         residual_ref, chunk_ref, scratch, end_ref) = refs
    core = lax.axis_index("c")

    @pl.when(core != lead)
    def _run():
        summed = tail_ref[...] + across_faces(faces_ref[...], far_ref[...], near_ref[...])
        end_ref[...] = apply_inverse(table_ref, scratch, right_ref[...] - summed)

    @pl.when(core == lead)
    def _keep():
        end_ref[...] = tail_ref[...]

    gain = gain_ref[...]
    residual = end_ref[...]
    if not sourced:
        residual = residual - gain * shift_ref[...]
    residual_ref[...] = residual
    rows = VALUES // 2
    chunk = packed(swap_halves(gain * swap_halves(residual) + residual))
    if sourced:
        gains = packed(gain * swap_halves(gain))
    for q in range(count):
        chunk_ref[q, :rows] = chunk
        if sourced:
            chunk_ref[q, rows:] = gains


def scanned(count, sums_ref, gains_ref):
    mine = lax.axis_index("q")
    rows = VALUES // 2
    before = jnp.zeros((rows, LANES), F32)
    for q in range(count):
        after = gains_ref[q, rows:] * before + sums_ref[q, :rows]
        before = jnp.where(q < mine, after, before)
    return unpacked(before)


def shifted(before, gain, residual):
    return jnp.where(low_half(), before, swap_halves(gain * before + residual))


def restart_kernel(lead, sums_ref, end_ref, gain_ref, table_ref, field_ref, scratch):
    @pl.when(lax.axis_index("c") == lead)
    def _field():
        before = scanned(sums_ref.shape[0], sums_ref, sums_ref)
        shift = shifted(before, gain_ref[...], end_ref[...])
        field_ref[...] = apply_inverse(table_ref, scratch, shift)

    @pl.when(lax.axis_index("c") != lead)
    def _later():
        field_ref[...] = jnp.zeros(FIELD, F32)


def late_restart_kernel(lead, field_ref, sums_ref, end_ref, gain_ref, faces_ref, table_ref, field_out,
                        ahead_ref, shift_ref, coarse_ref, scratch):
    gain, end = gain_ref[...], end_ref[...]
    shift = shifted(scanned(sums_ref.shape[0], sums_ref, sums_ref), gain, end)
    shift_ref[...] = shift
    coarse_ref[...] = gain * shift + end
    late_kernel(lead, field_ref, shift_ref, faces_ref, table_ref, field_out, ahead_ref, scratch)


def finish_kernel(count, sums_ref, gains_ref, residual_ref, gain_ref, coarse_ref, end_ref, out_ref, _):
    core = lax.axis_index("c")
    low = low_half()
    gain, residual = gain_ref[...], residual_ref[...]
    shift = shifted(scanned(count, sums_ref, gains_ref), gain, residual)
    end = coarse_ref[...] + (gain * shift + residual)
    end_ref[...] = end
    out_ref[...] = jnp.where(
        core == 0,
        jnp.where(low, swap_halves(end), residual),
        jnp.where(low, end, swap_halves(residual)),
    )


def output_kernel(end_ref, residual_ref, got_ref, place_ref, end_out, residual_out, _):
    core = lax.axis_index("c")
    low = low_half()
    got = got_ref[...]
    turned = swap_halves(got)
    end, residual = end_ref[...], residual_ref[...]
    end = jnp.where(core == 0, jnp.where(low, end, turned), jnp.where(low, got, end))
    residual = jnp.where(
        core == 0, jnp.where(low, residual, got), jnp.where(low, turned, residual)
    )
    place = place_ref[0:1, :]
    end_out[0] = columns(end, place)
    residual_out[0] = columns(residual, place)


def body(count, depth, initial_state, forcing, coarse_gain, block_inverse, face_blocks, neighbor, send_rows):
    def swap_cores(x):
        return lax.ppermute(x, "c", [(0, 1), (1, 0)])

    def halo(x, to):
        if to == 1:
            across = [(z + 1, depth + z) for z in range(depth - 1)]
        else:
            across = [(depth + z, z + 1) for z in range(depth - 1)]
        far = lax.ppermute(x, ("c", "space"), across)
        near = lax.ppermute(x, "c", [(1 - to, to)])
        return vmem(near), vmem(far)

    lead, other = 0, 1
    field, pair_shape = (FIELD, F32), ((2,) + FIELD, F32)
    index = ((8, LANES), jnp.int32)
    square_shape = ((VALUES,) + FIELD, F32)
    own, sent, start, mine, place, *raw = call(
        share_kernel, "share",
        [((STEPS + 1,) + FIELD, F32), ((STEPS // 2 + 1,) + FIELD, F32), field, index, index,
         (face_blocks.shape, F32), ((VALUES - EARLY,) + FIELD, F32), square_shape],
        *map(hbm, (neighbor, forcing, coarse_gain, initial_state, face_blocks, block_inverse)),
        fetch=True, scratch=(FIELD, forcing.shape, coarse_gain.shape, (EARLY,) + FIELD), ints=(neighbor.shape,),
    )
    got = swap_cores(sent)
    faces, table = call(
        tables_kernel, "tables",
        [((2 * VALUES, 6 * VALUES), BF16), square_shape], *map(vmem, (mine, *raw)), alias={3: 1},
    )
    operator = faces, table = vmem(faces), vmem(table)
    sources, gain, begun, right = call(
        functools.partial(first_kernel, lead), "first", [((STEPS,) + FIELD, F32), field, field, field],
        vmem(own), vmem(got), vmem(start), table,
    )
    sources, gain = vmem(sources), vmem(gain)

    def evolve(now, right=None, restart=(), squared=None):
        sourced = squared is None
        now = vmem(now)
        near, far = halo(now, other)
        if sourced:
            right = vmem(right)
            now, ahead = call(
                functools.partial(late_kernel, lead), "late", [field] * 2, now, right, *operator
            )
        else:
            now, ahead, right, coarse = call(
                functools.partial(late_restart_kernel, lead), "late", [field] * 4, now, *restart,
                *operator,
            )
            right = shift = vmem(right)
        (pair,) = call(
            functools.partial(open_kernel, lead), "open", [pair_shape],
            vmem(now), right, vmem(ahead), near, far, *operator,
        )
        for stage in range(STAGES - 1):
            active = (lead, other)[stage % 2]
            pair = vmem(pair)
            near, far = halo(pair, active)
            if sourced:
                ahead, squared = call(
                    functools.partial(ahead_square_kernel, active, stage // 2 * SQUARED), "ahead",
                    [field, square_shape], pair, *operator, *(() if stage == 0 else (squared,)),
                    alias={} if stage == 0 else {3: 1},
                )
                squared = vmem(squared)
            else:
                left = active == other and stage < STAGES - 2
                ahead, right = call(
                    functools.partial(ahead_right_kernel, active, left), "ahead", [field] * 2,
                    pair, right, *operator,
                )
                right = vmem(right)
            ahead = vmem(ahead)
            args = pair, right, ahead, near, far, *operator
            if stage < STAGES - 2:
                if sourced:
                    pair, right = call(
                        functools.partial(advance_kernel, stage, active, True), "advance",
                        [pair_shape, field], *args, sources,
                    )
                else:
                    pair, right = call(
                        functools.partial(advance_squared_kernel, stage, active), "advance",
                        [pair_shape, field], *args, squared, scratch=(FIELD, FIELD),
                    )
                right = vmem(right)
        (now,) = call(functools.partial(last_kernel, lead), "last", [field], *args)
        now = vmem(now)
        args = now, right, near, far, *operator
        near, far = halo(now, other)
        if sourced:
            tail, squared = call(
                functools.partial(tail_kernel, lead, VALUES - SQUARED), "tail",
                [field, square_shape], *args, squared, alias={6: 1},
            )
        else:
            (tail,) = call(functools.partial(tail_kernel, lead, None), "tail", [field], *args)
        rows = VALUES if sourced else VALUES // 2
        residual, chunk = call(
            functools.partial(ends_kernel, lead, sourced, count), "ends",
            [field, ((count, rows, LANES), F32)],
            right, vmem(tail), near, far, *operator, gain, *(() if sourced else (shift,)),
            scratch=(FIELD, FIELD),
        )
        gathered = vmem(lax.all_to_all(chunk, "q", 0, 0))
        return vmem(residual), gathered, vmem(squared) if sourced else coarse

    end, gains, squared = evolve(begun, right)
    restart = gains, end, gain
    (begun,) = call(
        functools.partial(restart_kernel, lead), "restart", [field], *restart, table
    )
    residual, sums, coarse = evolve(begun, restart=restart, squared=squared)
    end, sent = call(
        functools.partial(finish_kernel, count), "finish", [field, field],
        sums, gains, residual, gain, vmem(coarse),
    )
    got = vmem(swap_cores(sent))
    return call(
        output_kernel, "output", [((1,) + FIELD, F32)] * 2, vmem(end), residual, got, vmem(place),
        keep=False,
    )


def solution(mesh):
    slices, depth = mesh.devices.shape
    count = slices // 2
    pairs = Mesh(mesh.devices.reshape(count, 2, depth), ("q", "c", "space"))
    tm = ("q", "c")
    return jax.shard_map(
        functools.partial(body, count, depth),
        mesh=pairs,
        in_specs=(
            P(None, "space"),
            P(tm, None, "space"),
            P(tm, None, "space"),
            P(None, None, "space"),
            P(),
            P(None, "space"),
            P(None, "space"),
        ),
        out_specs=(P(tm, None, "space"), P(tm, None, "space")),
        check_vma=False,
    )
```

```python
import functools

import jax
import jax.numpy as jnp
from jax import lax
from jax.experimental import pallas as pl
from jax.experimental.pallas import tpu as pltpu
from jax.sharding import Mesh, PartitionSpec as P


VALUES = 64
LANES = 128
HALF = 64
STEPS = 4
STAGES = 2 * STEPS
GX = 8
GY = 8
SQUARED = 16
EARLY = 8
F32 = jnp.float32
BF16 = jnp.bfloat16
FIELD = (VALUES, LANES)


def vmem(x):
    return pltpu.with_memory_space_constraint(x, pltpu.VMEM)


def hbm(x):
    return pltpu.with_memory_space_constraint(x, pltpu.HBM)


def call(kernel, name, outs, *args, keep=True, fetch=False, alias={}, scratch=(FIELD,), ints=(), flops=1 << 22):
    whole = pl.BlockSpec(memory_space=pltpu.VMEM)
    shapes = tuple(
        pltpu.VMEM(shape, dtype) if keep else jax.ShapeDtypeStruct(shape, dtype)
        for shape, dtype in outs
    )
    held = [pltpu.VMEM(shape, F32) for shape in scratch]
    held += [pltpu.VMEM(shape, jnp.int32) for shape in ints]
    if fetch:
        held += [pltpu.SemaphoreType.DMA((16,))]
    return pl.pallas_call(
        kernel,
        out_shape=shapes,
        in_specs=[pl.BlockSpec(memory_space=pl.ANY) if fetch else whole] * len(args),
        out_specs=(whole,) * len(shapes),
        scratch_shapes=held,
        input_output_aliases=alias,
        cost_estimate=pl.CostEstimate(flops=flops, bytes_accessed=1 << 20, transcendentals=0),
        compiler_params=pltpu.CompilerParams(vmem_limit_bytes=16 << 20),
        name=name,
    )(*args)


def low_half():
    return lax.broadcasted_iota(jnp.int32, FIELD, 1) < HALF


def swap_halves(x):
    return pltpu.roll(x, HALF, 1)


def columns(x, index):
    return jnp.take_along_axis(x, jnp.broadcast_to(index, x.shape), axis=1)


def raster(neighbor):
    ahead = jnp.concatenate([neighbor, jnp.zeros((2, LANES), jnp.int32)], axis=0)
    level = jnp.where(ahead[4:5, :] >= LANES, 0, HALF)
    steps = (ahead >= 0).astype(jnp.int32)
    span = 1
    while span < max(GX, GY):
        on = ahead >= 0
        spot = jnp.clip(ahead, 0, LANES - 1)
        steps = steps + jnp.where(on, jnp.take_along_axis(steps, spot, axis=1), 0)
        ahead = jnp.where(on, jnp.take_along_axis(ahead, spot, axis=1), -1)
        span *= 2
    place = level + GX * steps[2:3, :] + steps[0:1, :]
    down = jnp.transpose(jnp.broadcast_to(place.astype(F32), (LANES, LANES)))
    across = lax.broadcasted_iota(jnp.int32, (LANES, LANES), 1).astype(F32)
    at = lax.broadcasted_iota(jnp.int32, (LANES, LANES), 0).astype(F32)
    order = jnp.sum(jnp.where(down == across, at, 0.0), axis=0, keepdims=True).astype(jnp.int32)
    return jnp.broadcast_to(place, (8, LANES)), jnp.broadcast_to(order, (8, LANES))


def apply_inverse(inverse_ref, scratch, vector):
    scratch[...] = vector
    total = inverse_ref[0] * scratch[0:1, :]
    for j in range(1, VALUES):
        total = total + inverse_ref[j] * scratch[j : j + 1, :]
    return total


def halves(x):
    high = x.astype(BF16)
    return high, (x - high.astype(F32)).astype(BF16)


def product(faces, layers):
    width = layers.shape[1]
    parts = jnp.dot(faces, jnp.concatenate(halves(layers), axis=1), preferred_element_type=F32)
    upper, lower = parts[:VALUES], parts[VALUES:]
    return upper[:, :width] + ((upper[:, width:] + lower[:, :width]) + lower[:, width:])


def own_faces(field, faces):
    lane = lax.broadcasted_iota(jnp.int32, FIELD, 1)
    x = jnp.bitwise_and(lane, GX - 1)
    y = jnp.bitwise_and(lane, GX * GY - GX)
    picked = [
        jnp.where(inside, pltpu.roll(field, by % LANES, 1), 0.0)
        for inside, by in ((x > 0, 1), (x < GX - 1, -1), (y > 0, GX), (y < GX * GY - GX, -GX))
    ]
    return product(faces[:, : 4 * VALUES], jnp.concatenate(picked, axis=0))


def share_kernel(neighbor_any, forcing_any, gain_any, state_any, blocks_any, inverse_any,
                 own_ref, out_ref, start_ref, mine_ref, place_ref, blocks_ref, rest_ref, table_ref,
                 state_ref, forcing_ref, gain_ref, early_ref, neighbor_ref, sems):
    core = lax.axis_index("c")
    part = VALUES // 8
    first = [
        pltpu.make_async_copy(neighbor_any, neighbor_ref, sems.at[0]),
        pltpu.make_async_copy(forcing_any, forcing_ref, sems.at[1]),
        pltpu.make_async_copy(gain_any, gain_ref, sems.at[2]),
        pltpu.make_async_copy(state_any, state_ref, sems.at[3]),
    ]
    early, later = (
        [
            pltpu.make_async_copy(
                inverse_any.at[pl.ds(begin + part * k, part)], ref.at[pl.ds(part * k, part)],
                sems.at[8 + begin // part + k],
            )
            for k in range(count)
        ]
        for begin, ref, count in (
            (0, early_ref, EARLY // part), (EARLY, rest_ref, (VALUES - EARLY) // part)
        )
    )
    later.append(pltpu.make_async_copy(blocks_any, blocks_ref, sems.at[4]))
    for copy in first + early + later:
        copy.start()
    first[0].wait()
    place, order = raster(neighbor_ref[...])
    turned = pltpu.roll(order, HALF, 1)
    low = lax.broadcasted_iota(jnp.int32, (8, LANES), 1) < HALF
    lowest, highest = jnp.where(low, order, turned), jnp.where(low, turned, order)
    mine = jnp.where(core == 0, lowest, highest)
    other = jnp.where(core == 0, highest, lowest)
    mine_ref[...] = mine
    place_ref[...] = place
    mine, other = mine[0:1, :], other[0:1, :]
    for copy in first[1:]:
        copy.wait()
    fields = [forcing_ref[m] for m in range(STEPS)] + [gain_ref[0]]
    for m in range(0, STEPS, 2):
        out_ref[m // 2] = jnp.where(
            low_half(), columns(fields[m], other), columns(fields[m + 1], other)
        )
    out_ref[STEPS // 2] = columns(fields[STEPS], other)
    for m, field in enumerate(fields):
        own_ref[m] = columns(field, mine)
    start_ref[...] = columns(state_ref[...], mine)
    for k, copy in enumerate(early):
        copy.wait()
        rows = pl.ds(part * k, part)
        for j in range(VALUES):
            table_ref[j, rows] = columns(early_ref[rows, j, :], mine)
    for copy in later:
        copy.wait()


def tables_kernel(mine_ref, blocks_ref, rest_ref, _table, faces_ref, table_ref, _):
    core = lax.axis_index("c")
    mine = jnp.concatenate([mine_ref[...]] * ((VALUES - EARLY) // 8), axis=0)
    blocks = [blocks_ref[f] for f in range(4)]
    blocks += [
        jnp.where(core == 0, blocks_ref[4], blocks_ref[5]),
        jnp.where(core == 0, blocks_ref[5], blocks_ref[4]),
    ]
    for f, block in enumerate(blocks):
        high, low = halves(block)
        faces_ref[:VALUES, f * VALUES : (f + 1) * VALUES] = high
        faces_ref[VALUES:, f * VALUES : (f + 1) * VALUES] = low
    for j in range(VALUES):
        table_ref[j, EARLY:] = columns(rest_ref[:, j, :], mine)


def packed(x):
    rows = VALUES // 2
    return jnp.where(low_half()[:rows], x[:rows], swap_halves(x)[rows:])


def unpacked(x):
    low, turned = low_half()[: VALUES // 2], swap_halves(x)
    return jnp.concatenate([jnp.where(low, x, turned), jnp.where(low, turned, x)], axis=0)


def first_kernel(
    lead, own_ref, got_ref, start_ref, table_ref, sources_ref, gain_ref, field_ref, right_ref, scratch
):
    core = lax.axis_index("c")
    low = low_half()
    is_own = low == (core == 0)
    for m in range(STEPS + 1):
        got = got_ref[m // 2]
        turned = swap_halves(got)
        if m % 2 == 0:
            other = jnp.where(core == 0, turned, got)
        else:
            other = jnp.where(core == 0, got, turned)
        value = jnp.where(is_own, own_ref[m], other)
        if m < STEPS:
            sources_ref[m] = value
        else:
            gain_ref[...] = value
    first = jnp.logical_and(low, lax.axis_index("q") == 0)
    right = jnp.where(first, start_ref[...], 0.0) + sources_ref[0]
    right_ref[...] = right
    begin(lead, right, table_ref, field_ref, scratch)


def begin(lead, right, table_ref, field_ref, scratch):
    @pl.when(lax.axis_index("c") == lead)
    def _field():
        field_ref[...] = apply_inverse(table_ref, scratch, right)

    @pl.when(lax.axis_index("c") != lead)
    def _later():
        field_ref[...] = jnp.zeros(FIELD, F32)


def late_kernel(lead, field_ref, right_ref, faces_ref, table_ref, field_out,
                ahead_ref, scratch):
    core = lax.axis_index("c")

    @pl.when(core != lead)
    def _run():
        field = apply_inverse(table_ref, scratch, right_ref[...])
        field_out[...] = field
        ahead_ref[...] = own_faces(field, faces_ref[...])

    @pl.when(core == lead)
    def _keep():
        field_out[...] = field_ref[...]


def ahead_right_kernel(active, left, pair_ref, right_ref, faces_ref, table_ref, ahead_ref, right_out, scratch):
    @pl.when(lax.axis_index("c") == active)
    def _run():
        ahead_ref[...] = own_faces(pair_ref[1], faces_ref[...])
        right_out[...] = right_ref[...]

    @pl.when(lax.axis_index("c") != active)
    def _right():
        if left:
            right_out[...] = apply_inverse(table_ref, scratch, right_ref[...])
        else:
            right_out[...] = right_ref[...]


def square(begin, table_ref, square_ref, scratch):
    @pl.loop(begin, begin + SQUARED)
    def _column(j):
        square_ref[j] = apply_inverse(table_ref, scratch, table_ref[j])


def ahead_square_kernel(active, begin, pair_ref, faces_ref, table_ref, *refs):
    ahead_ref, square_ref, scratch = refs[-3:]

    @pl.when(lax.axis_index("c") == active)
    def _run():
        ahead_ref[...] = own_faces(pair_ref[1], faces_ref[...])
        square(begin, table_ref, square_ref, scratch)


def across_faces(faces, far, near):
    return product(faces[:, 4 * VALUES :], jnp.concatenate([far, near], axis=0))


def open_kernel(lead, field_ref, right_ref, ahead_ref, near_ref, far_ref, faces_ref, table_ref,
                pair_out, scratch):
    core = lax.axis_index("c")

    @pl.when(core != lead)
    def _run():
        summed = ahead_ref[...] + across_faces(faces_ref[...], far_ref[...], near_ref[...])
        pair_out[0] = field_ref[...]
        pair_out[1] = apply_inverse(table_ref, scratch, right_ref[...] - summed)

    @pl.when(core == lead)
    def _keep():
        pair_out[0] = jnp.zeros(FIELD, F32)
        pair_out[1] = field_ref[...]


def advance_kernel(stage, active, sourced, pair_ref, right_ref, ahead_ref, near_ref, far_ref,
                   faces_ref, table_ref, sources_ref, pair_out, right_out,
                   scratch):
    core = lax.axis_index("c")

    @pl.when(core == active)
    def _run():
        faces = faces_ref[...]
        far, near = (jnp.concatenate([ref[0], ref[1]], axis=1) for ref in (far_ref, near_ref))
        across = across_faces(faces, far, near)
        right = right_ref[...]

        def taken(summed, right, stage):
            field = apply_inverse(table_ref, scratch, right - summed)
            if stage % 2 == 1:
                right = field
                if sourced:
                    right = right + sources_ref[(stage + 1) // 2]
                field = apply_inverse(table_ref, scratch, right)
            return field, right

        field, right = taken(ahead_ref[...] + across[:, :LANES], right, stage)
        pair_out[0] = field
        summed = own_faces(field, faces) + across[:, LANES:]
        field, right = taken(summed, right, stage + 1)
        pair_out[1] = field
        right_out[...] = right

    @pl.when(core != active)
    def _keep():
        pair_out[...] = pair_ref[...]
        right_out[...] = right_ref[...]


def advance_squared_kernel(stage, active, pair_ref, right_ref, ahead_ref, near_ref, far_ref,
                           faces_ref, table_ref, square_ref, pair_out, right_out, scratch, other):
    core = lax.axis_index("c")

    @pl.when(core == active)
    def _run():
        faces = faces_ref[...]
        far, near = (jnp.concatenate([ref[0], ref[1]], axis=1) for ref in (far_ref, near_ref))
        across = across_faces(faces, far, near)
        right = right_ref[...]
        vector = right - (ahead_ref[...] + across[:, :LANES])
        if stage % 2 == 0:
            field = apply_inverse(table_ref, scratch, vector)
            pair_out[0] = field
            vector = right - (own_faces(field, faces) + across[:, LANES:])
            pair_out[1] = apply_inverse(square_ref, other, vector)
            right_out[...] = vector
        else:
            field = apply_inverse(square_ref, scratch, vector)
            pair_out[0] = field
            right = apply_inverse(table_ref, scratch, vector)
            right_out[...] = right
            vector = right - (own_faces(field, faces) + across[:, LANES:])
            pair_out[1] = apply_inverse(table_ref, other, vector)

    @pl.when(core != active)
    def _keep():
        pair_out[...] = pair_ref[...]
        right_out[...] = right_ref[...]


def last_kernel(lead, pair_ref, right_ref, ahead_ref, near_ref, far_ref, faces_ref, table_ref,
                field_out, scratch):
    core = lax.axis_index("c")

    @pl.when(core == lead)
    def _run():
        summed = ahead_ref[...] + across_faces(faces_ref[...], far_ref[0], near_ref[0])
        field_out[...] = apply_inverse(table_ref, scratch, right_ref[...] - summed)

    @pl.when(core != lead)
    def _keep():
        field_out[...] = pair_ref[1]


def tail_kernel(lead, begin, field_ref, right_ref, near_ref, far_ref, faces_ref, table_ref, *refs):
    if begin is None:
        out_ref, scratch = refs
    else:
        _, out_ref, square_ref, scratch = refs
    core = lax.axis_index("c")
    out_ref[...] = own_faces(field_ref[...], faces_ref[...])

    @pl.when(core == lead)
    def _run():
        summed = out_ref[...] + across_faces(faces_ref[...], far_ref[1], near_ref[1])
        out_ref[...] = apply_inverse(table_ref, scratch, right_ref[...] - summed)

    if begin is not None:
        @pl.when(core != lead)
        def _square():
            square(begin, table_ref, square_ref, scratch)


def ends_kernel(lead, sourced, count, *refs):
    if sourced:
        (right_ref, tail_ref, near_ref, far_ref, faces_ref, table_ref, gain_ref, residual_ref,
         chunk_ref, scratch, end_ref) = refs
    else:
        (right_ref, tail_ref, near_ref, far_ref, faces_ref, table_ref, gain_ref, shift_ref,
         residual_ref, chunk_ref, scratch, end_ref) = refs
    core = lax.axis_index("c")

    @pl.when(core != lead)
    def _run():
        summed = tail_ref[...] + across_faces(faces_ref[...], far_ref[...], near_ref[...])
        end_ref[...] = apply_inverse(table_ref, scratch, right_ref[...] - summed)

    @pl.when(core == lead)
    def _keep():
        end_ref[...] = tail_ref[...]

    gain = gain_ref[...]
    residual = end_ref[...]
    if not sourced:
        residual = residual - gain * shift_ref[...]
    residual_ref[...] = residual
    rows = VALUES // 2
    chunk = packed(swap_halves(gain * swap_halves(residual) + residual))
    if sourced:
        gains = packed(gain * swap_halves(gain))
    for q in range(count):
        chunk_ref[q, :rows] = chunk
        if sourced:
            chunk_ref[q, rows:] = gains


def scanned(count, sums_ref, gains_ref):
    mine = lax.axis_index("q")
    rows = VALUES // 2
    before = jnp.zeros((rows, LANES), F32)
    for q in range(count):
        after = gains_ref[q, rows:] * before + sums_ref[q, :rows]
        before = jnp.where(q < mine, after, before)
    return unpacked(before)


def shifted(before, gain, residual):
    return jnp.where(low_half(), before, swap_halves(gain * before + residual))


def restart_kernel(lead, sums_ref, end_ref, gain_ref, table_ref, field_ref, scratch):
    @pl.when(lax.axis_index("c") == lead)
    def _field():
        before = scanned(sums_ref.shape[0], sums_ref, sums_ref)
        shift = shifted(before, gain_ref[...], end_ref[...])
        field_ref[...] = apply_inverse(table_ref, scratch, shift)

    @pl.when(lax.axis_index("c") != lead)
    def _later():
        field_ref[...] = jnp.zeros(FIELD, F32)


def late_restart_kernel(lead, field_ref, sums_ref, end_ref, gain_ref, faces_ref, table_ref, field_out,
                        ahead_ref, shift_ref, coarse_ref, scratch):
    gain, end = gain_ref[...], end_ref[...]
    shift = shifted(scanned(sums_ref.shape[0], sums_ref, sums_ref), gain, end)
    shift_ref[...] = shift
    coarse_ref[...] = gain * shift + end
    late_kernel(lead, field_ref, shift_ref, faces_ref, table_ref, field_out, ahead_ref, scratch)


def finish_kernel(count, sums_ref, gains_ref, residual_ref, gain_ref, coarse_ref, end_ref, out_ref, _):
    core = lax.axis_index("c")
    low = low_half()
    gain, residual = gain_ref[...], residual_ref[...]
    shift = shifted(scanned(count, sums_ref, gains_ref), gain, residual)
    end = coarse_ref[...] + (gain * shift + residual)
    end_ref[...] = end
    out_ref[...] = jnp.where(
        core == 0,
        jnp.where(low, swap_halves(end), residual),
        jnp.where(low, end, swap_halves(residual)),
    )


def output_kernel(end_ref, residual_ref, got_ref, place_ref, end_out, residual_out, _):
    core = lax.axis_index("c")
    low = low_half()
    got = got_ref[...]
    turned = swap_halves(got)
    end, residual = end_ref[...], residual_ref[...]
    end = jnp.where(core == 0, jnp.where(low, end, turned), jnp.where(low, got, end))
    residual = jnp.where(
        core == 0, jnp.where(low, residual, got), jnp.where(low, turned, residual)
    )
    place = place_ref[0:1, :]
    end_out[0] = columns(end, place)
    residual_out[0] = columns(residual, place)


def body(count, depth, initial_state, forcing, coarse_gain, block_inverse, face_blocks, neighbor, send_rows):
    def swap_cores(x):
        return lax.ppermute(x, "c", [(0, 1), (1, 0)])

    def halo(x, to):
        if to == 1:
            across = [(z + 1, depth + z) for z in range(depth - 1)]
        else:
            across = [(depth + z, z + 1) for z in range(depth - 1)]
        far = lax.ppermute(x, ("c", "space"), across)
        near = lax.ppermute(x, "c", [(1 - to, to)])
        return vmem(near), vmem(far)

    lead, other = 0, 1
    field, pair_shape = (FIELD, F32), ((2,) + FIELD, F32)
    index = ((8, LANES), jnp.int32)
    square_shape = ((VALUES,) + FIELD, F32)
    own, sent, start, mine, place, *raw = call(
        share_kernel, "share",
        [((STEPS + 1,) + FIELD, F32), ((STEPS // 2 + 1,) + FIELD, F32), field, index, index,
         (face_blocks.shape, F32), ((VALUES - EARLY,) + FIELD, F32), square_shape],
        *map(hbm, (neighbor, forcing, coarse_gain, initial_state, face_blocks, block_inverse)),
        fetch=True, scratch=(FIELD, forcing.shape, coarse_gain.shape, (EARLY,) + FIELD), ints=(neighbor.shape,),
    )
    got = swap_cores(sent)
    faces, table = call(
        tables_kernel, "tables",
        [((2 * VALUES, 6 * VALUES), BF16), square_shape], *map(vmem, (mine, *raw)), alias={3: 1},
    )
    operator = faces, table = vmem(faces), vmem(table)
    sources, gain, begun, right = call(
        functools.partial(first_kernel, lead), "first", [((STEPS,) + FIELD, F32), field, field, field],
        vmem(own), vmem(got), vmem(start), table,
    )
    sources, gain = vmem(sources), vmem(gain)

    def evolve(now, right=None, restart=(), squared=None):
        sourced = squared is None
        now = vmem(now)
        near, far = halo(now, other)
        if sourced:
            right = vmem(right)
            now, ahead = call(
                functools.partial(late_kernel, lead), "late", [field] * 2, now, right, *operator
            )
        else:
            now, ahead, right, coarse = call(
                functools.partial(late_restart_kernel, lead), "late", [field] * 4, now, *restart,
                *operator,
            )
            right = shift = vmem(right)
        (pair,) = call(
            functools.partial(open_kernel, lead), "open", [pair_shape],
            vmem(now), right, vmem(ahead), near, far, *operator,
        )
        for stage in range(STAGES - 1):
            active = (lead, other)[stage % 2]
            pair = vmem(pair)
            near, far = halo(pair, active)
            if sourced:
                ahead, squared = call(
                    functools.partial(ahead_square_kernel, active, stage // 2 * SQUARED), "ahead",
                    [field, square_shape], pair, *operator, *(() if stage == 0 else (squared,)),
                    alias={} if stage == 0 else {3: 1},
                )
                squared = vmem(squared)
            else:
                left = active == other and stage < STAGES - 2
                ahead, right = call(
                    functools.partial(ahead_right_kernel, active, left), "ahead", [field] * 2,
                    pair, right, *operator,
                )
                right = vmem(right)
            ahead = vmem(ahead)
            args = pair, right, ahead, near, far, *operator
            if stage < STAGES - 2:
                if sourced:
                    pair, right = call(
                        functools.partial(advance_kernel, stage, active, True), "advance",
                        [pair_shape, field], *args, sources,
                    )
                else:
                    pair, right = call(
                        functools.partial(advance_squared_kernel, stage, active), "advance",
                        [pair_shape, field], *args, squared, scratch=(FIELD, FIELD),
                    )
                right = vmem(right)
        (now,) = call(functools.partial(last_kernel, lead), "last", [field], *args)
        now = vmem(now)
        args = now, right, near, far, *operator
        near, far = halo(now, other)
        if sourced:
            tail, squared = call(
                functools.partial(tail_kernel, lead, VALUES - SQUARED), "tail",
                [field, square_shape], *args, squared, alias={6: 1},
            )
        else:
            (tail,) = call(functools.partial(tail_kernel, lead, None), "tail", [field], *args)
        rows = VALUES if sourced else VALUES // 2
        residual, chunk = call(
            functools.partial(ends_kernel, lead, sourced, count), "ends",
            [field, ((count, rows, LANES), F32)],
            right, vmem(tail), near, far, *operator, gain, *(() if sourced else (shift,)),
            scratch=(FIELD, FIELD),
        )
        gathered = vmem(lax.all_to_all(chunk, "q", 0, 0))
        return vmem(residual), gathered, vmem(squared) if sourced else coarse

    end, gains, squared = evolve(begun, right)
    restart = gains, end, gain
    (begun,) = call(
        functools.partial(restart_kernel, lead), "restart", [field], *restart, table
    )
    residual, sums, coarse = evolve(begun, restart=restart, squared=squared)
    end, sent = call(
        functools.partial(finish_kernel, count), "finish", [field, field],
        sums, gains, residual, gain, vmem(coarse),
    )
    got = vmem(swap_cores(sent))
    return call(
        output_kernel, "output", [((1,) + FIELD, F32)] * 2, vmem(end), residual, got, vmem(place),
        keep=False,
    )


def solution(mesh):
    slices, depth = mesh.devices.shape
    count = slices // 2
    pairs = Mesh(mesh.devices.reshape(count, 2, depth), ("q", "c", "space"))
    tm = ("q", "c")
    return jax.shard_map(
        functools.partial(body, count, depth),
        mesh=pairs,
        in_specs=(
            P(None, "space"),
            P(tm, None, "space"),
            P(tm, None, "space"),
            P(None, None, "space"),
            P(),
            P(None, "space"),
            P(None, "space"),
        ),
        out_specs=(P(tm, None, "space"), P(tm, None, "space")),
        check_vma=False,
    )
```
